32 devices in a mesh: groups: 2 (over y), space: 8 (over z, x), tm: 2 (over core).
Axes of the slice: x: 2, y: 2, z: 4, core: 2. Of those that a mesh axis runs over, the one named last changes fastest.
Arguments:
- latents: bfloat16 [4, 16, 4, 256, 256], P('groups', 'space', 'tm'), parts along dimension 0, may hold values from -6 to 6
- cotangent: bfloat16 [4, 16, 4, 256, 256], P('groups', 'space', 'tm'), parts along dimension 0, may hold values from -6 to 6
- valid_frames: int32 [4], P('groups'), parts along dimension 0, may hold values from 1 to 16, as said below
- spatial_weight: bfloat16 [9, 256, 256], replicated, may hold values from -0.125 to 0.125
- temporal_weight: bfloat16 [3, 256, 256], replicated, may hold values from -0.21875 to 0.21875
- cond_weight: bfloat16 [256, 256], replicated, may hold values from -0.375 to 0.375
Outputs:
- output: bfloat16 [4, 16, 4, 256, 256], P('groups', 'space', 'tm'), parts along dimension 0
- grad_latents: bfloat16 [4, 16, 4, 256, 256], P('groups', 'space', 'tm'), parts along dimension 0
- grad_spatial: bfloat16 [18, 256, 256], P('groups'), parts along dimension 0
- grad_temporal: bfloat16 [6, 256, 256], P('groups'), parts along dimension 0
- grad_cond: bfloat16 [512, 256], P('groups'), parts along dimension 0
The draws below stay inside these ranges and needn't reach their ends.
There are 2 independent parts, one for each index of `groups`. The reference program is written for one: setup_inputs(seed, part) draws one part's arguments, and reference() takes and returns one part's arrays. A program takes and returns all parts, laid end to end along the dimension named above; an argument that names none is the same for every part. Nothing has to cross between parts.
Inputs may be any that keep to these rules, and one draw needn't show every extreme that they name: `valid_frames`: the first clip has all 16 frames valid; the others have 1 to 16.
All inputs are finite; a program needn't handle non-finite values.
Results may differ from the reference program's by a relative error of at most 0.0055.
Values may be sent and summed in bfloat16 or wider, within the bound.
A program may use at most 128 MiB of HBM per device.

```python
import jax
import jax.numpy as jnp
from jax import lax

C = 256
CLIPS = 2
WIDTH = 256
FRAMES = 16
HEIGHT = 4


def draw_valid_frames(key, part):
    lengths = jax.random.randint(key, (CLIPS,), 1, FRAMES + 1)
    return jnp.where(jnp.arange(CLIPS) == 0, FRAMES, lengths).astype(jnp.int32)


def levels(own_key, shape, split, low, high):
    def one(dim, shards_of):
        draws = jax.random.uniform(jax.random.fold_in(jax.random.fold_in(own_key, 6), dim), (shards_of,), jnp.float32, low / len(split), high / len(split))
        return jnp.repeat(jnp.exp(draws), shape[dim] // shards_of).reshape((-1,) + (1,) * (len(shape) - dim - 1))

    factor_of = one(*split[0])
    for cut in split[1:]:
        factor_of = factor_of * one(*cut)
    return factor_of


def bell_draw(key, extent, scale, bound, cuts=(), kind=jnp.bfloat16):
    drawn = jax.random.normal(key, extent, jnp.float32) * scale
    if len(cuts) > 0:
        drawn = levels(key, extent, cuts, -0.22, 0.18) * drawn
    return jnp.clip(drawn, min=-bound, max=bound).astype(kind)


def setup_inputs(seed: int = 0, part: int = 0) -> dict:
    key_list = jax.random.split(jax.random.key(seed), 7)
    part_keys = jax.random.split(jax.random.fold_in(key_list[6], part), 7)
    return {
        "latents": bell_draw(part_keys[0], (CLIPS, FRAMES, HEIGHT, WIDTH, C), 1.0, 6.0, ((1, 8), (2, 2))),
        "cotangent": bell_draw(part_keys[1], (CLIPS, FRAMES, HEIGHT, WIDTH, C), 1.0, 6.0, ((1, 8), (2, 2))),
        "valid_frames": draw_valid_frames(jax.random.fold_in(jax.random.fold_in(key_list[6], part), 71), part),
        "spatial_weight": bell_draw(key_list[3], (9, C, C), (9 * C) ** -0.5, 0.125),
        "temporal_weight": bell_draw(key_list[4], (3, C, C), (3 * C) ** -0.5, 0.21875),
        "cond_weight": bell_draw(key_list[5], (C, C), C ** -0.5, 0.375),
    }


def spatial_sum(padded, weights, flip):
    rows = padded.shape[2] - 2
    cols = padded.shape[3] - 2
    total = jnp.zeros(padded.shape[:2] + (rows, cols, weights.shape[2]), jnp.float32)
    for row_off in range(3):
        for col_off in range(3):
            if flip:
                piece = padded[:, :, 2 - row_off:2 - row_off + rows, 2 - col_off:2 - col_off + cols]
                kernel = weights[3 * row_off + col_off].T
            else:
                piece = padded[:, :, row_off:row_off + rows, col_off:col_off + cols]
                kernel = weights[3 * row_off + col_off]
            total = total + jnp.dot(piece, kernel, preferred_element_type=jnp.float32)
    return total


def reference(latents, cotangent, valid_frames, spatial_weight, temporal_weight, cond_weight):
    frame_ids = jnp.arange(FRAMES, dtype=jnp.int32)
    mask = (frame_ids[None, :] < valid_frames[:, None]).astype(jnp.bfloat16)[:, :, None, None, None]
    masked = latents * mask
    padded = jnp.pad(masked, ((0, 0), (0, 0), (1, 1), (1, 1), (0, 0)))
    pre = spatial_sum(padded, spatial_weight, False)
    act = jax.nn.silu(pre).astype(jnp.bfloat16)
    act_pad = jnp.pad(act, ((0, 0), (2, 0), (0, 0), (0, 0), (0, 0)))
    mixed = jnp.zeros(pre.shape, jnp.float32)
    for lag in range(3):
        mixed = mixed + jnp.dot(act_pad[:, 2 - lag:2 - lag + FRAMES], temporal_weight[lag], preferred_element_type=jnp.float32)
    cond = jnp.dot(masked[:, 0], cond_weight, preferred_element_type=jnp.float32)
    output = ((masked.astype(jnp.float32) + mixed + cond[:, None]) * mask.astype(jnp.float32)).astype(jnp.bfloat16)

    cot = cotangent * mask
    cot_pad = jnp.pad(cot, ((0, 0), (0, 2), (0, 0), (0, 0), (0, 0)))
    dact = jnp.zeros(pre.shape, jnp.float32)
    for lag in range(3):
        dact = dact + jnp.dot(cot_pad[:, lag:lag + FRAMES], temporal_weight[lag].T, preferred_element_type=jnp.float32)
    sig = jax.nn.sigmoid(pre)
    dpre = (dact * sig * (1.0 + pre * (1.0 - sig))).astype(jnp.bfloat16)
    cot_sum = jnp.sum(cot.astype(jnp.float32), axis=1)
    cond_back = jnp.dot(cot_sum, cond_weight.astype(jnp.float32).T, precision=lax.Precision.HIGHEST)
    dpre_pad = jnp.pad(dpre, ((0, 0), (0, 0), (1, 1), (1, 1), (0, 0)))
    dmasked = spatial_sum(dpre_pad, spatial_weight, True)
    first = (frame_ids == 0).astype(jnp.float32)[None, :, None, None, None]
    grad_latents = ((cot.astype(jnp.float32) + dmasked + first * cond_back[:, None]) * mask.astype(jnp.float32)).astype(jnp.bfloat16)

    scale = (CLIPS * FRAMES * HEIGHT * WIDTH) ** -0.5
    dims = (((0, 1, 2, 3), (0, 1, 2, 3)), ((), ()))
    spatial_terms = []
    for row_off in range(3):
        for col_off in range(3):
            piece = padded[:, :, row_off:row_off + HEIGHT, col_off:col_off + WIDTH]
            spatial_terms.append(lax.dot_general(piece, dpre, dims, preferred_element_type=jnp.float32))
    grad_spatial = (jnp.stack(spatial_terms) * scale).astype(jnp.bfloat16)
    temporal_terms = []
    for lag in range(3):
        temporal_terms.append(lax.dot_general(act_pad[:, 2 - lag:2 - lag + FRAMES], cot, dims, preferred_element_type=jnp.float32))
    grad_temporal = (jnp.stack(temporal_terms) * scale).astype(jnp.bfloat16)
    grad_cond = lax.dot_general(masked[:, 0].astype(jnp.float32), cot_sum, (((0, 1, 2), (0, 1, 2)), ((), ())), precision=lax.Precision.HIGHEST)
    grad_cond = (grad_cond * scale).astype(jnp.bfloat16)
    return output, grad_latents, grad_spatial, grad_temporal, grad_cond
```

```python
import jax
import jax.numpy as jnp
from jax import lax
from jax.sharding import PartitionSpec as P


def broadcast_first(value, axis):
    count = lax.axis_size(axis)
    me = lax.axis_index(axis)
    step = 1
    while step < count:
        pairs = [(i, i + step) for i in range(step) if i + step < count]
        got = lax.ppermute(value, axis, pairs)
        value = jnp.where((me >= step) & (me < 2 * step), got, value)
        step *= 2
    return value


def reduce_first(value, axis):
    count = lax.axis_size(axis)
    step = 1
    while step < count:
        step *= 2
    step //= 2
    while step >= 1:
        pairs = [(i + step, i) for i in range(step) if i + step < count]
        got = lax.ppermute(value.astype(jnp.bfloat16), axis, pairs)
        value = value + got.astype(jnp.float32)
        step //= 2
    return value


def swap(value, axis, bit):
    count = lax.axis_size(axis)
    return lax.ppermute(value, axis, [(i, i ^ bit) for i in range(count)])


def sum_all(value, order):
    sides = []
    for axis, bit in order:
        side = (lax.axis_index(axis) // bit) % 2
        half = value.shape[0] // 2
        low, high = value[:half], value[half:]
        mine = jnp.where(side == 0, low, high)
        other = jnp.where(side == 0, high, low).astype(jnp.bfloat16)
        value = mine + swap(other, axis, bit).astype(jnp.float32)
        sides.append(side)
    value = value.astype(jnp.bfloat16)
    for (axis, bit), side in zip(reversed(order), reversed(sides)):
        got = swap(value, axis, bit)
        value = jnp.where(
            side == 0,
            jnp.concatenate([value, got], axis=0),
            jnp.concatenate([got, value], axis=0),
        )
    return value


def shifted(value, axis, by):
    count = lax.axis_size(axis)
    pairs = [(i, i + by) for i in range(count) if 0 <= i + by < count]
    return lax.ppermute(value, axis, pairs)


def spatial_sum(padded, weights, flip):
    rows = padded.shape[2] - 2
    cols = padded.shape[3] - 2
    total = jnp.zeros(padded.shape[:2] + (rows, cols, weights.shape[2]), jnp.float32)
    for row_off in range(3):
        for col_off in range(3):
            if flip:
                piece = padded[
                    :, :, 2 - row_off : 2 - row_off + rows, 2 - col_off : 2 - col_off + cols
                ]
                kernel = weights[3 * row_off + col_off].T
            else:
                piece = padded[:, :, row_off : row_off + rows, col_off : col_off + cols]
                kernel = weights[3 * row_off + col_off]
            total = total + jnp.dot(piece, kernel, preferred_element_type=jnp.float32)
    return total


def lag_forward(padded_act, weights, count):
    total = 0.0
    for lag in range(3):
        total = total + jnp.dot(
            padded_act[:, 2 - lag : 2 - lag + count],
            weights[lag],
            preferred_element_type=jnp.float32,
        )
    return total


def lag_backward(padded_cot, weights, count):
    total = 0.0
    for lag in range(3):
        total = total + jnp.dot(
            padded_cot[:, lag : lag + count], weights[lag].T, preferred_element_type=jnp.float32
        )
    return total


DIMS = (((0, 1, 2, 3), (0, 1, 2, 3)), ((), ()))


def outer(left, right):
    return lax.dot_general(left, right, DIMS, preferred_element_type=jnp.float32)


def with_halo(value):
    low = shifted(value[:, :, -1:], "tm", 1)
    high = shifted(value[:, :, :1], "tm", -1)
    rows = jnp.concatenate([low, value, high], axis=2)
    return jnp.pad(rows, ((0, 0), (0, 0), (0, 0), (1, 1), (0, 0)))


def on_device(latents, cotangent, valid_frames, spatial_weight, temporal_weight, cond_weight):
    clips, frames, rows, cols, chans = latents.shape
    slab = lax.axis_index("space")
    frame_ids = slab * frames + jnp.arange(frames, dtype=jnp.int32)
    mask = (frame_ids[None, :] < valid_frames[:, None]).astype(jnp.bfloat16)[:, :, None, None, None]
    mask_f = mask.astype(jnp.float32)
    masked = latents * mask
    cot = cotangent * mask
    padded = with_halo(masked)
    later = shifted(cot, "space", -1)
    first = broadcast_first(masked[:, 0], "space")
    cot_sum = reduce_first(jnp.sum(cot, axis=1, dtype=jnp.float32), "space")
    pre = spatial_sum(padded, spatial_weight, False)
    act = jax.nn.silu(pre).astype(jnp.bfloat16)
    earlier = shifted(act, "space", 1)
    cot_pad = jnp.concatenate([cot, later], axis=1)
    dact = lag_backward(cot_pad, temporal_weight, frames)
    sig = jax.nn.sigmoid(pre)
    dpre = (dact * sig * (1.0 + pre * (1.0 - sig))).astype(jnp.bfloat16)
    dpre_pad = with_halo(dpre)
    terms = []
    for row_off in range(3):
        for col_off in range(3):
            piece = padded[:, :, row_off : row_off + rows, col_off : col_off + cols]
            terms.append(outer(piece, dpre))
    for lag in range(3):
        terms.append(outer(act, cot_pad[:, lag : lag + frames]))
    wide_first = jnp.broadcast_to(first[:, None], cot.shape)
    terms.append(outer(wide_first, cot))
    space = lax.axis_size("space")
    bits = [1 << k for k in range(1, space.bit_length() - 1)]
    order = [("tm", 1)] + [("space", bit) for bit in bits] + [("space", 1)]
    grads = sum_all(jnp.concatenate(terms, axis=0), order)
    dmasked = spatial_sum(dpre_pad, spatial_weight, True)
    cond_back = jnp.dot(cot_sum, cond_weight.astype(jnp.float32).T, precision=lax.Precision.HIGHEST)
    is_first = (frame_ids == 0).astype(jnp.float32)[None, :, None, None, None]
    grad_latents = (
        (cot.astype(jnp.float32) + dmasked + is_first * cond_back[:, None]) * mask_f
    ).astype(jnp.bfloat16)
    act_pad = jnp.concatenate([earlier, act], axis=1)
    mixed = lag_forward(act_pad, temporal_weight, frames)
    cond = jnp.dot(first, cond_weight, preferred_element_type=jnp.float32)
    output = ((masked.astype(jnp.float32) + mixed + cond[:, None]) * mask_f).astype(jnp.bfloat16)
    scale = (clips * frames * rows * cols * lax.axis_size("space") * lax.axis_size("tm")) ** (-0.5)
    scaled = (grads.astype(jnp.float32) * scale).astype(jnp.bfloat16)
    scaled = scaled.reshape(13, chans, chans)
    return (output, grad_latents, scaled[:9], scaled[9:12], scaled[12])


def solution(mesh):
    return jax.shard_map(
        on_device,
        mesh=mesh,
        in_specs=(
            P("groups", "space", "tm", None, None),
            P("groups", "space", "tm", None, None),
            P("groups"),
            P(),
            P(),
            P(),
        ),
        out_specs=(
            P("groups", "space", "tm", None, None),
            P("groups", "space", "tm", None, None),
            P("groups", None, None),
            P("groups", None, None),
            P("groups", None),
        ),
        check_vma=False,
    )
```

```python
import functools

import jax
import jax.numpy as jnp
from jax import lax
from jax.experimental import pallas as pl
from jax.experimental.pallas import tpu as pltpu
from jax.sharding import PartitionSpec as P

MESH = pl.DeviceIdType.MESH
BF = jnp.bfloat16
F32 = jnp.float32


def nn(left, right):
    return jnp.dot(left, right, preferred_element_type=F32)


def nt(left, right):
    return lax.dot_general(left, right, (((1,), (1,)), ((), ())), preferred_element_type=F32)


def bits_of(count):
    far = []
    bit = 2
    while bit < count:
        far.append(bit)
        bit *= 2
    return far + ([1] if count > 1 else [])


def kernel(n, dims, scale, *refs):
    clips, frames, rows, cols, chans, sizes = dims
    (lat, cotan, mask, sw, tw, cw, out, glat, gsp, gtm, gcd,
     xm, xh, x3, xt, pre, actp, at, cotp, dm, dh, fst, ft, csum, cs, cr, cb,
     acc, tmr, xs, xr, ms, zs, zr, res,
     halo_sem, cot_sem, act_sem, first_sem, sum_sem, tm_sem, x_sem, z_send, z_recv,
     g_send, g_recv, xg_sem, tg_sem) = refs
    d3 = x3
    group = lax.axis_index("groups")
    s = lax.axis_index("space")
    c = lax.axis_index("tm")
    half = n // 2
    xb = lax.rem(s, 2)
    q = lax.div(s, 2)
    pos = rows * cols
    order = bits_of(n)
    levels = len(order)

    def at_dev(space, core):
        return (group, space, core)

    def copy(src, dst, sems, dev):
        return pltpu.make_async_remote_copy(
            src_ref=src, dst_ref=dst, send_sem=sems[0], recv_sem=sems[1],
            device_id=dev, device_id_type=MESH)

    def pair(sem, *index):
        return sem.at[(0,) + index], sem.at[(1,) + index]

    partner = at_dev(s, 1 - c)
    side = at_dev(s + 1 - 2 * xb, c)

    barrier = pltpu.get_barrier_semaphore()
    pl.semaphore_signal(barrier, inc=1, device_id=partner, device_id_type=MESH)
    for d in range(1, n):
        pl.semaphore_signal(
            barrier, inc=1, device_id=at_dev(lax.rem(s + d, n), c), device_id_type=MESH)
    pl.semaphore_wait(barrier, n)

    def mask_of(b, t):
        return mask[b * frames + t]

    for b in range(clips):
        for t in range(frames):
            cotp[b, t] = (cotan[b, t].astype(F32) * mask_of(b, t)).astype(BF)

    def cot_copy(b):
        return copy(cotp.at[b, pl.ds(0, frames)], cotp.at[b, pl.ds(frames, frames)],
                    pair(cot_sem, b), at_dev(jnp.maximum(s - 1, 0), c))

    def act_copy(b):
        return copy(actp.at[b, pl.ds(frames, frames)], actp.at[b, pl.ds(0, frames)],
                    pair(act_sem, b), at_dev(jnp.minimum(s + 1, n - 1), c))

    @pl.when(s > 0)
    def _():
        for b in range(clips):
            cot_copy(b).start()

    for b in range(clips):
        for t in range(frames):
            xm[b * frames + t] = (lat[b, t].astype(F32) * mask_of(b, t)).astype(BF)

    edge = pl.ds(pl.multiple_of((1 - c) * (rows - 1) * cols, cols), cols)
    x_halo = copy(xm.at[:, edge], xh, pair(halo_sem, 0), partner)
    x_halo.start()
    d_halo = copy(dm.at[:, edge], dh, pair(halo_sem, 1), partner)

    def clear(upto):
        held = jnp.bool_(True)
        for bit in upto:
            held = held & (lax.rem(lax.div(s, bit), 2) == 0)
        return held

    def has(bit):
        return lax.rem(lax.div(s, bit), 2) == 1

    out_order = order[::-1]

    def first_copy(level):
        bit = out_order[level]
        return copy(fst, fst, pair(first_sem, level), at_dev(jnp.minimum(s + bit, n - 1), c))

    def first_send(level):
        @pl.when(clear(out_order[level:]))
        def _():
            first_copy(level).start()

    def first_recv(level):
        @pl.when(has(out_order[level]) & clear(out_order[level + 1:]))
        def _():
            first_copy(level).wait_recv()

    def first_done(level):
        @pl.when(clear(out_order[level:]))
        def _():
            first_copy(level).wait_send()

    def sum_copy(level):
        return copy(cs, cr.at[level], pair(sum_sem, level),
                    at_dev(jnp.maximum(s - order[level], 0), c))

    def sum_send(level):
        @pl.when(has(order[level]) & clear(order[:level]))
        def _():
            cs[...] = csum[...].astype(BF)
            sum_copy(level).start()

    def sum_recv(level):
        @pl.when(clear(order[:level + 1]))
        def _():
            sum_copy(level).wait_recv()
            csum[...] += cr[level].astype(F32)

    def sum_done(level):
        @pl.when(has(order[level]) & clear(order[:level]))
        def _():
            sum_copy(level).wait_send()

    @pl.when(s == 0)
    def _():
        for b in range(clips):
            fst[b] = xm[b * frames]

    first_send(0)
    for b in range(clips):
        total = cotp[b, 0].astype(F32)
        for t in range(1, frames):
            total += cotp[b, t].astype(F32)
        csum[b] = total
    sum_send(0)

    @pl.when(s == n - 1)
    def _():
        cotp[:, frames:] = jnp.zeros((clips, frames, pos, chans), BF)

    @pl.when(s == 0)
    def _():
        actp[:, :frames] = jnp.zeros((clips, frames, pos, chans), BF)

    ids = lax.broadcasted_iota(jnp.int32, (cols, chans), 0)

    def spread(dst, bt, block, value, flip):
        wide = value.astype(F32)
        prev = jnp.where(ids == 0, 0.0, pltpu.roll(wide, 1, 0)).astype(BF)
        nxt = jnp.where(ids == cols - 1, 0.0, pltpu.roll(wide, cols - 1, 0)).astype(BF)
        span = pl.ds(pl.multiple_of(block * cols, cols), cols)
        lo, hi = (nxt, prev) if flip else (prev, nxt)
        dst[bt, span, 0:chans] = lo
        dst[bt, span, chans:2 * chans] = value
        dst[bt, span, 2 * chans:3 * chans] = hi

    def spread_own(dst, src, flip):
        @pl.loop(0, clips * frames)
        def _(bt):
            for r in range(rows):
                spread(dst, bt, r + 1, src[bt, r * cols:(r + 1) * cols], flip)

    def spread_halo(dst, src, flip):
        @pl.loop(0, clips * frames)
        def _(bt):
            got = src[bt].astype(F32)
            spread(dst, bt, 0, (got * c.astype(F32)).astype(BF), flip)
            spread(dst, bt, rows + 1, (got * (1 - c).astype(F32)).astype(BF), flip)

    spread_own(x3, xm, False)

    @pl.loop(0, clips * frames)
    def _(bt):
        xt[bt] = xm[bt].T

    x_halo.wait()
    spread_halo(x3, xh, False)

    for b in range(clips):
        @pl.loop(0, frames)
        def _(t):
            bt = b * frames + t
            total = nn(x3[bt, 0:pos], sw[0])
            for i in range(1, 3):
                total += nn(x3[bt, i * cols:i * cols + pos], sw[i])
            pre[bt] = total
            act = (total * jax.nn.sigmoid(total)).astype(BF)
            actp[b, frames + t] = act
            at[bt] = act.T

    first_recv(0)
    if levels > 1:
        first_send(1)
    sum_recv(0)
    if levels > 1:
        sum_send(1)

    for b in range(clips):
        @pl.when(s < n - 1)
        def _():
            cot_copy(b).wait_recv()

        @pl.when(s < n - 1)
        def _():
            act_copy(b).start()

        @pl.loop(0, frames)
        def _(t):
            bt = b * frames + t
            dact = nt(cotp[b, t], tw[0])
            for k in range(1, 3):
                dact += nt(cotp[b, t + k], tw[k])
            value = pre[bt]
            sig = jax.nn.sigmoid(value)
            dm[bt] = (dact * sig * (1.0 + value * (1.0 - sig))).astype(BF)

    d_halo.start()
    for level in range(1, levels):
        first_recv(level)
        if level + 1 < levels:
            first_send(level + 1)

    base = [sum(sizes[:k]) for k in range(len(sizes))]

    def part(k, div, index, count):
        size = sizes[k] // div
        return pl.ds(pl.multiple_of(index * size, 16), size * count)

    def shift(k, div, offset):
        size = sizes[k] // div
        return pl.ds(pl.multiple_of(base[k] // div + offset, 16), size)

    def tm_copy(k):
        size = sizes[k] // 2
        src = acc.at[pl.ds(pl.multiple_of(base[k] + (1 - c) * size, 16), size)]
        return copy(src, tmr.at[pl.ds(base[k] // 2, size)], pair(tm_sem, k), partner)

    def x_copy(k):
        span = pl.ds(base[k] // 4, sizes[k] // 4)
        return copy(xs.at[span], xr.at[span], pair(x_sem, k), side)

    def z_peer(d):
        other = lax.rem(q + d, half)
        return other, at_dev(2 * other + xb, c)

    def z_copy(k, d):
        size = sizes[k] // (2 * n)
        other, dev = z_peer(d)
        src = zs.at[pl.ds(pl.multiple_of(base[k] // 4 + other * size, 16), size)]
        dst = zr.at[d - 1, pl.ds(base[k] // (2 * n), size)]
        return copy(src, dst, (z_send.at[k, d - 1], z_recv.at[k, d - 1]), dev)

    def quarter(k):
        return base[k] + c * (sizes[k] // 2) + xb * (sizes[k] // 4)

    def g_copy(k, d, place):
        size = sizes[k] // (2 * n)
        own = res.at[pl.ds(pl.multiple_of(quarter(k) + place * size, 16), size)]
        return copy(own, own, (g_send.at[k, d - 1], g_recv.at[k, d - 1]), z_peer(d)[1])

    def xg_copy(k, bit):
        size = sizes[k] // 4
        start = base[k] + c * (sizes[k] // 2) + bit * size
        own = res.at[pl.ds(pl.multiple_of(start, 16), size)]
        return copy(own, own, pair(xg_sem, k), side)

    def tg_copy(k, bit):
        size = sizes[k] // 2
        own = res.at[pl.ds(pl.multiple_of(base[k] + bit * size, 16), size)]
        return copy(own, own, pair(tg_sem, k), partner)

    def stage_x(k):
        tm_copy(k).wait_recv()
        size = sizes[k] // 4
        away = (1 - xb) * size
        xs[pl.ds(base[k] // 4, size)] = (
            acc[pl.ds(pl.multiple_of(base[k] + c * 2 * size + away, 16), size)]
            + tmr[pl.ds(pl.multiple_of(base[k] // 2 + away, 16), size)]).astype(BF)
        x_copy(k).start()

    def stage_z(k):
        x_copy(k).wait_recv()
        size = sizes[k] // 4
        span = pl.ds(base[k] // 4, size)
        total = (acc[pl.ds(pl.multiple_of(quarter(k), 16), size)]
                 + tmr[pl.ds(pl.multiple_of(base[k] // 2 + xb * size, 16), size)]
                 + xr[span].astype(F32))
        ms[span] = total
        zs[span] = total.astype(BF)
        for d in range(1, half):
            z_copy(k, d).start()

    def stage_g(k):
        size = sizes[k] // (2 * n)
        total = ms[pl.ds(pl.multiple_of(base[k] // 4 + q * size, 16), size)]
        for d in range(1, half):
            z_copy(k, d).wait_recv()
            total += zr[d - 1, pl.ds(base[k] // (2 * n), size)].astype(F32)
        res[pl.ds(pl.multiple_of(quarter(k) + q * size, 16), size)] = (total * scale).astype(BF)
        for d in range(1, half):
            g_copy(k, d, q).start()

    def stage_xg(k):
        for d in range(1, half):
            g_copy(k, d, lax.rem(q + half - d, half)).wait_recv()
        xg_copy(k, xb).start()

    def stage_tg(k):
        xg_copy(k, 1 - xb).wait_recv()
        tg_copy(k, c).start()

    def stage_end(k):
        tg_copy(k, 1 - c).wait_recv()

    def write_tap(k, tap, value):
        acc[base[k] + tap * chans:base[k] + (tap + 1) * chans] = value

    for b in range(clips):
        ft[b] = fst[b].T
    for k in range(3):
        total = jnp.zeros((chans, chans), F32)
        for b in range(clips):
            for t in range(frames):
                total += nn(at[b * frames + t], cotp[b, t + k])
        write_tap(0, k, total)
    total = jnp.zeros((chans, chans), F32)
    for b in range(clips):
        for t in range(frames):
            total += nn(ft[b], cotp[b, t])
    write_tap(0, 3, total)
    for k in range(4):
        used = (4 if k == 0 else 3) * chans
        if sizes[k] > used:
            acc[base[k] + used:base[k] + sizes[k]] = jnp.zeros((sizes[k] - used, chans), F32)
    tm_copy(0).start()

    spread_own(d3, dm, True)
    d_halo.wait()
    spread_halo(d3, dh, True)
    stage_x(0)

    def spatial_grad(i):
        for j in range(3):
            total = jnp.zeros((chans, chans), F32)
            for bt in range(clips * frames):
                piece = d3[bt, (2 - i) * cols:(2 - i) * cols + pos, j * chans:(j + 1) * chans]
                total += nn(xt[bt], piece)
            write_tap(1 + i, j, total)
        tm_copy(1 + i).start()

    spatial_grad(0)
    stage_z(0)
    spatial_grad(1)
    stage_x(1)
    spatial_grad(2)
    stage_x(2)
    stage_z(1)
    stage_x(3)
    stage_g(0)
    stage_z(2)

    for level in range(1, levels):
        sum_recv(level)
        if level + 1 < levels:
            sum_send(level + 1)

    @pl.when(s == 0)
    def _():
        for b in range(clips):
            high = csum[b].astype(BF)
            low = (csum[b] - high.astype(F32)).astype(BF)
            cb[b] = nt(high, cw[...]) + nt(low, cw[...])

    @pl.when(s > 0)
    def _():
        cb[...] = jnp.zeros((clips, pos, chans), F32)

    def back(b, t):
        bt = b * frames + t
        total = cotp[b, t].astype(F32)
        for i in range(3):
            for j in range(3):
                piece = d3[bt, (2 - i) * cols:(2 - i) * cols + pos, j * chans:(j + 1) * chans]
                total += nt(piece, sw[i, j * chans:(j + 1) * chans])
        if t == 0:
            total += cb[b]
        glat[b, t] = (total * mask_of(b, t)).astype(BF)

    stage_z(3)
    stage_g(1)
    for b in range(clips):
        for t in range(frames):
            back(b, t)
    stage_xg(0)
    stage_g(2)
    stage_g(3)
    stage_xg(1)
    stage_tg(0)

    for b in range(clips):
        @pl.when(s > 0)
        def _():
            act_copy(b).wait_recv()
        cond = nn(fst[b], cw[...])
        for t in range(frames):
            total = xm[b * frames + t].astype(F32) + cond
            for k in range(3):
                total += nn(actp[b, frames + t - k], tw[k])
            out[b, t] = (total * mask_of(b, t)).astype(BF)

    stage_xg(2)
    stage_tg(1)
    stage_xg(3)
    stage_tg(2)
    stage_tg(3)
    for k in range(4):
        stage_end(k)
    gtm[...] = res[0:3 * chans]
    gcd[...] = res[3 * chans:4 * chans]
    for i in range(3):
        gsp[i * 3 * chans:(i + 1) * 3 * chans] = res[base[1 + i]:base[1 + i] + 3 * chans]

    for level in range(levels):
        first_done(level)
        sum_done(level)

    @pl.when(s > 0)
    def _():
        for b in range(clips):
            cot_copy(b).wait_send()

    @pl.when(s < n - 1)
    def _():
        for b in range(clips):
            act_copy(b).wait_send()

    for k in range(4):
        tm_copy(k).wait_send()
        x_copy(k).wait_send()
        for d in range(1, half):
            z_copy(k, d).wait_send()
            g_copy(k, d, q).wait_send()
        xg_copy(k, xb).wait_send()
        tg_copy(k, c).wait_send()


def on_device(latents, cotangent, valid_frames, spatial_weight, temporal_weight, cond_weight):
    clips, frames, rows, cols, chans = latents.shape
    n = lax.axis_size("space")
    slab = lax.axis_index("space")
    frame_ids = slab * frames + jnp.arange(frames, dtype=jnp.int32)
    mask = (frame_ids[None, :] < valid_frames[:, None]).astype(F32).reshape(clips * frames)
    scale = (clips * frames * rows * cols * n * lax.axis_size("tm")) ** (-0.5)
    pos = rows * cols
    unit = 32 * n
    sizes = [-(-taps * chans // unit) * unit for taps in (4, 3, 3, 3)]
    total = sum(sizes)
    bt = clips * frames
    levels = len(bits_of(n))
    half = n // 2
    dma = pltpu.SemaphoreType.DMA
    big = (clips, frames, pos, chans)
    scratch = [
        pltpu.VMEM((bt, pos, chans), BF),
        pltpu.VMEM((bt, cols, chans), BF),
        pltpu.VMEM((bt, pos + 2 * cols, 3 * chans), BF),
        pltpu.VMEM((bt, chans, pos), BF),
        pltpu.VMEM((bt, pos, chans), F32),
        pltpu.VMEM((clips, 2 * frames, pos, chans), BF),
        pltpu.VMEM((bt, chans, pos), BF),
        pltpu.VMEM((clips, 2 * frames, pos, chans), BF),
        pltpu.VMEM((bt, pos, chans), BF),
        pltpu.VMEM((bt, cols, chans), BF),
        pltpu.VMEM((clips, pos, chans), BF),
        pltpu.VMEM((clips, chans, pos), BF),
        pltpu.VMEM((clips, pos, chans), F32),
        pltpu.VMEM((clips, pos, chans), BF),
        pltpu.VMEM((levels, clips, pos, chans), BF),
        pltpu.VMEM((clips, pos, chans), F32),
        pltpu.VMEM((total, chans), F32),
        pltpu.VMEM((total // 2, chans), F32),
        pltpu.VMEM((total // 4, chans), BF),
        pltpu.VMEM((total // 4, chans), BF),
        pltpu.VMEM((total // 4, chans), F32),
        pltpu.VMEM((total // 4, chans), BF),
        pltpu.VMEM((half - 1, total // (2 * n), chans), BF),
        pltpu.VMEM((total, chans), BF),
        dma((2, 2)), dma((2, clips)), dma((2, clips)), dma((2, levels)), dma((2, levels)),
        dma((2, 4)), dma((2, 4)), dma((4, half - 1)), dma((4, half - 1)),
        dma((4, half - 1)), dma((4, half - 1)), dma((2, 4)), dma((2, 4)),
    ]
    vmem = pl.BlockSpec(memory_space=pltpu.VMEM)
    smem = pl.BlockSpec(memory_space=pltpu.SMEM)
    shape = jax.ShapeDtypeStruct
    outs = pl.pallas_call(
        functools.partial(kernel, n, (clips, frames, rows, cols, chans, sizes), scale),
        out_shape=[
            shape(big, BF), shape(big, BF), shape((9 * chans, chans), BF),
            shape((3 * chans, chans), BF), shape((chans, chans), BF)],
        in_specs=[vmem, vmem, smem, vmem, vmem, vmem],
        out_specs=[vmem] * 5,
        scratch_shapes=scratch,
        compiler_params=pltpu.CompilerParams(
            collective_id=0, has_side_effects=True, vmem_limit_bytes=58 * 2**20),
    )(
        latents.reshape(big), cotangent.reshape(big), mask,
        spatial_weight.reshape(3, 3 * chans, chans), temporal_weight, cond_weight)
    output, grad_latents, grad_spatial, grad_temporal, grad_cond = outs
    return (
        output.reshape(latents.shape), grad_latents.reshape(latents.shape),
        grad_spatial.reshape(9, chans, chans), grad_temporal.reshape(3, chans, chans), grad_cond)


def solution(mesh):
    return jax.shard_map(
        on_device,
        mesh=mesh,
        in_specs=(
            P("groups", "space", "tm", None, None),
            P("groups", "space", "tm", None, None),
            P("groups"),
            P(),
            P(),
            P(),
        ),
        out_specs=(
            P("groups", "space", "tm", None, None),
            P("groups", "space", "tm", None, None),
            P("groups", None, None),
            P("groups", None, None),
            P("groups", None),
        ),
        check_vma=False,
    )
```

```python
import functools

import jax
import jax.numpy as jnp
from jax import lax
from jax.experimental import pallas as pl
from jax.experimental.pallas import tpu as pltpu
from jax.sharding import PartitionSpec as P

MESH = pl.DeviceIdType.MESH
BF = jnp.bfloat16
F32 = jnp.float32


def nn(left, right):
    return jnp.dot(left, right, preferred_element_type=F32)


def nt(left, right):
    return lax.dot_general(left, right, (((1,), (1,)), ((), ())), preferred_element_type=F32)


def bits_of(count):
    far = []
    bit = 2
    while bit < count:
        far.append(bit)
        bit *= 2
    return far + ([1] if count > 1 else [])


def kernel(n, dims, scale, *refs):
    clips, frames, rows, cols, chans, sizes = dims
    (lat, cotan, mask, sw, tw, cw, out, glat, gsp, gtm, gcd,
     xm, xh, x3, xt, pre, actp, at, cotp, dm, dh, fst, ft, csum, cs, cr, cb,
     acc, tmr, xs, xr, ms, zs, zr, res,
     halo_sem, cot_sem, act_sem, first_sem, sum_sem, tm_sem, x_sem, z_send, z_recv,
     g_send, g_recv, xg_sem, tg_sem) = refs
    d3 = x3
    group = lax.axis_index("groups")
    s = lax.axis_index("space")
    c = lax.axis_index("tm")
    half = n // 2
    xb = lax.rem(s, 2)
    q = lax.div(s, 2)
    pos = rows * cols
    order = bits_of(n)
    levels = len(order)

    def at_dev(space, core):
        return (group, space, core)

    def copy(src, dst, sems, dev):
        return pltpu.make_async_remote_copy(
            src_ref=src, dst_ref=dst, send_sem=sems[0], recv_sem=sems[1],
            device_id=dev, device_id_type=MESH)

    def pair(sem, *index):
        return sem.at[(0,) + index], sem.at[(1,) + index]

    partner = at_dev(s, 1 - c)
    side = at_dev(s + 1 - 2 * xb, c)

    barrier = pltpu.get_barrier_semaphore()
    pl.semaphore_signal(barrier, inc=1, device_id=partner, device_id_type=MESH)
    for d in range(1, n):
        pl.semaphore_signal(
            barrier, inc=1, device_id=at_dev(lax.rem(s + d, n), c), device_id_type=MESH)
    pl.semaphore_wait(barrier, n)

    def mask_of(b, t):
        return mask[b * frames + t]

    for b in range(clips):
        for t in range(frames):
            cotp[b, t] = (cotan[b, t].astype(F32) * mask_of(b, t)).astype(BF)

    def cot_copy(b):
        return copy(cotp.at[b, pl.ds(0, frames)], cotp.at[b, pl.ds(frames, frames)],
                    pair(cot_sem, b), at_dev(jnp.maximum(s - 1, 0), c))

    def act_copy(b):
        return copy(actp.at[b, pl.ds(frames, frames)], actp.at[b, pl.ds(0, frames)],
                    pair(act_sem, b), at_dev(jnp.minimum(s + 1, n - 1), c))

    @pl.when(s > 0)
    def _():
        for b in range(clips):
            cot_copy(b).start()

    for b in range(clips):
        for t in range(frames):
            xm[b * frames + t] = (lat[b, t].astype(F32) * mask_of(b, t)).astype(BF)

    edge = pl.ds(pl.multiple_of((1 - c) * (rows - 1) * cols, cols), cols)
    x_halo = copy(xm.at[:, edge], xh, pair(halo_sem, 0), partner)
    x_halo.start()

    def d_halo(b):
        span = pl.ds(b * frames, frames)
        return copy(dm.at[span, edge], dh.at[span], pair(halo_sem, 1 + b), partner)

    def clear(upto):
        held = jnp.bool_(True)
        for bit in upto:
            held = held & (lax.rem(lax.div(s, bit), 2) == 0)
        return held

    def has(bit):
        return lax.rem(lax.div(s, bit), 2) == 1

    out_order = order[::-1]

    def first_copy(level, b):
        return copy(fst.at[b], fst.at[b], pair(first_sem, level, b),
                    at_dev(jnp.minimum(s + out_order[level], n - 1), c))

    def first_send(level, b):
        @pl.when(clear(out_order[level:]))
        def _():
            first_copy(level, b).start()

    def first_recv(level, b):
        @pl.when(has(out_order[level]) & clear(out_order[level + 1:]))
        def _():
            first_copy(level, b).wait_recv()

    def first_done(level, b):
        @pl.when(clear(out_order[level:]))
        def _():
            first_copy(level, b).wait_send()

    def sum_copy(level, b):
        return copy(cs.at[b], cr.at[level, b], pair(sum_sem, level, b),
                    at_dev(jnp.maximum(s - order[level], 0), c))

    def sum_send(level, b):
        @pl.when(has(order[level]) & clear(order[:level]))
        def _():
            cs[b] = csum[b].astype(BF)
            sum_copy(level, b).start()

    def sum_recv(level, b):
        @pl.when(clear(order[:level + 1]))
        def _():
            sum_copy(level, b).wait_recv()
            csum[b] += cr[level, b].astype(F32)

    def sum_done(level, b):
        @pl.when(has(order[level]) & clear(order[:level]))
        def _():
            sum_copy(level, b).wait_send()

    hops = sorted(((level, b) for level in range(levels) for b in range(clips)),
                  key=lambda hop: (hop[0] + hop[1], hop[0]))

    def serve(count):
        for _ in range(min(count, len(hops))):
            level, b = hops.pop(0)
            first_recv(level, b)
            sum_recv(level, b)
            if level + 1 < levels:
                first_send(level + 1, b)
                sum_send(level + 1, b)

    @pl.when(s == 0)
    def _():
        for b in range(clips):
            fst[b] = xm[b * frames]

    for b in range(clips):
        first_send(0, b)
        total = cotp[b, 0].astype(F32)
        for t in range(1, frames):
            total += cotp[b, t].astype(F32)
        csum[b] = total
        sum_send(0, b)

    @pl.when(s == n - 1)
    def _():
        cotp[:, frames:] = jnp.zeros((clips, frames, pos, chans), BF)

    @pl.when(s == 0)
    def _():
        actp[:, :frames] = jnp.zeros((clips, frames, pos, chans), BF)

    ids = lax.broadcasted_iota(jnp.int32, (cols, chans), 0)

    def spread(dst, bt, block, value, flip):
        wide = value.astype(F32)
        prev = jnp.where(ids == 0, 0.0, pltpu.roll(wide, 1, 0)).astype(BF)
        nxt = jnp.where(ids == cols - 1, 0.0, pltpu.roll(wide, cols - 1, 0)).astype(BF)
        span = pl.ds(pl.multiple_of(block * cols, cols), cols)
        lo, hi = (nxt, prev) if flip else (prev, nxt)
        dst[bt, span, 0:chans] = lo
        dst[bt, span, chans:2 * chans] = value
        dst[bt, span, 2 * chans:3 * chans] = hi

    def spread_own(dst, src, flip, begin, end):
        @pl.loop(begin, end)
        def _(bt):
            for r in range(rows):
                spread(dst, bt, r + 1, src[bt, r * cols:(r + 1) * cols], flip)

    def spread_halo(dst, src, flip, begin, end):
        @pl.loop(begin, end)
        def _(bt):
            got = src[bt].astype(F32)
            spread(dst, bt, 0, (got * c.astype(F32)).astype(BF), flip)
            spread(dst, bt, rows + 1, (got * (1 - c).astype(F32)).astype(BF), flip)

    spread_own(x3, xm, False, 0, clips * frames)

    @pl.loop(0, clips * frames)
    def _(bt):
        xt[bt] = xm[bt].T

    x_halo.wait()
    spread_halo(x3, xh, False, 0, clips * frames)

    for b in range(clips):
        @pl.loop(0, frames)
        def _(t):
            bt = b * frames + t
            total = nn(x3[bt, 0:pos], sw[0])
            for i in range(1, 3):
                total += nn(x3[bt, i * cols:i * cols + pos], sw[i])
            pre[bt] = total
            act = (total * jax.nn.sigmoid(total)).astype(BF)
            actp[b, frames + t] = act
            at[bt] = act.T

    serve(1)

    base = [sum(sizes[:k]) for k in range(len(sizes))]

    def part(k, div, index, count):
        size = sizes[k] // div
        return pl.ds(pl.multiple_of(index * size, 16), size * count)

    def shift(k, div, offset):
        size = sizes[k] // div
        return pl.ds(pl.multiple_of(base[k] // div + offset, 16), size)

    def tm_copy(k):
        size = sizes[k] // 2
        src = acc.at[pl.ds(pl.multiple_of(base[k] + (1 - c) * size, 16), size)]
        return copy(src, tmr.at[pl.ds(base[k] // 2, size)], pair(tm_sem, k), partner)

    def x_copy(k):
        span = pl.ds(base[k] // 4, sizes[k] // 4)
        return copy(xs.at[span], xr.at[span], pair(x_sem, k), side)

    def z_peer(d):
        other = lax.rem(q + d, half)
        return other, at_dev(2 * other + xb, c)

    def z_copy(k, d):
        size = sizes[k] // (2 * n)
        other, dev = z_peer(d)
        src = zs.at[pl.ds(pl.multiple_of(base[k] // 4 + other * size, 16), size)]
        dst = zr.at[d - 1, pl.ds(base[k] // (2 * n), size)]
        return copy(src, dst, (z_send.at[k, d - 1], z_recv.at[k, d - 1]), dev)

    def quarter(k):
        return base[k] + c * (sizes[k] // 2) + xb * (sizes[k] // 4)

    def g_copy(k, d, place):
        size = sizes[k] // (2 * n)
        own = res.at[pl.ds(pl.multiple_of(quarter(k) + place * size, 16), size)]
        return copy(own, own, (g_send.at[k, d - 1], g_recv.at[k, d - 1]), z_peer(d)[1])

    def xg_copy(k, bit):
        size = sizes[k] // 4
        start = base[k] + c * (sizes[k] // 2) + bit * size
        own = res.at[pl.ds(pl.multiple_of(start, 16), size)]
        return copy(own, own, pair(xg_sem, k), side)

    def tg_copy(k, bit):
        size = sizes[k] // 2
        own = res.at[pl.ds(pl.multiple_of(base[k] + bit * size, 16), size)]
        return copy(own, own, pair(tg_sem, k), partner)

    def stage_x(k):
        tm_copy(k).wait_recv()
        size = sizes[k] // 4
        away = (1 - xb) * size
        xs[pl.ds(base[k] // 4, size)] = (
            acc[pl.ds(pl.multiple_of(base[k] + c * 2 * size + away, 16), size)]
            + tmr[pl.ds(pl.multiple_of(base[k] // 2 + away, 16), size)]).astype(BF)
        x_copy(k).start()

    def stage_z(k):
        x_copy(k).wait_recv()
        size = sizes[k] // 4
        span = pl.ds(base[k] // 4, size)
        total = (acc[pl.ds(pl.multiple_of(quarter(k), 16), size)]
                 + tmr[pl.ds(pl.multiple_of(base[k] // 2 + xb * size, 16), size)]
                 + xr[span].astype(F32))
        ms[span] = total
        zs[span] = total.astype(BF)
        for d in range(1, half):
            z_copy(k, d).start()

    def stage_g(k):
        size = sizes[k] // (2 * n)
        total = ms[pl.ds(pl.multiple_of(base[k] // 4 + q * size, 16), size)]
        for d in range(1, half):
            z_copy(k, d).wait_recv()
            total += zr[d - 1, pl.ds(base[k] // (2 * n), size)].astype(F32)
        res[pl.ds(pl.multiple_of(quarter(k) + q * size, 16), size)] = (total * scale).astype(BF)
        for d in range(1, half):
            g_copy(k, d, q).start()

    def stage_xg(k):
        for d in range(1, half):
            g_copy(k, d, lax.rem(q + half - d, half)).wait_recv()
        xg_copy(k, xb).start()

    def stage_tg(k):
        xg_copy(k, 1 - xb).wait_recv()
        tg_copy(k, c).start()

    def stage_end(k):
        tg_copy(k, 1 - c).wait_recv()

    def add_tap(k, tap, value, b):
        span = slice(base[k] + tap * chans, base[k] + (tap + 1) * chans)
        if b == 0:
            acc[span] = value
        else:
            acc[span] += value

    for k, taps in enumerate((3, 3, 3, 3, 1)):
        if sizes[k] > taps * chans:
            acc[base[k] + taps * chans:base[k] + sizes[k]] = jnp.zeros(
                (sizes[k] - taps * chans, chans), F32)

    def spatial_grad(b, i):
        for j in range(3):
            total = jnp.zeros((chans, chans), F32)
            for bt in range(b * frames, (b + 1) * frames):
                piece = d3[bt, (2 - i) * cols:(2 - i) * cols + pos, j * chans:(j + 1) * chans]
                total += nn(xt[bt], piece)
            add_tap(1 + i, j, total, b)

    def back_sum(b, t):
        bt = b * frames + t
        total = cotp[b, t].astype(F32)
        for i in range(3):
            for j in range(3):
                piece = d3[bt, (2 - i) * cols:(2 - i) * cols + pos, j * chans:(j + 1) * chans]
                total += nt(piece, sw[i, j * chans:(j + 1) * chans])
        return total

    for b in range(clips):
        @pl.when(s < n - 1)
        def _():
            cot_copy(b).wait_recv()

        if b == clips - 1:
            @pl.when(s < n - 1)
            def _():
                for each in range(clips):
                    act_copy(each).start()

        @pl.loop(0, frames)
        def _(t):
            bt = b * frames + t
            dact = nt(cotp[b, t], tw[0])
            for k in range(1, 3):
                dact += nt(cotp[b, t + k], tw[k])
            value = pre[bt]
            sig = jax.nn.sigmoid(value)
            dm[bt] = (dact * sig * (1.0 + value * (1.0 - sig))).astype(BF)

        d_halo(b).start()
        for k in range(3):
            total = jnp.zeros((chans, chans), F32)
            for t in range(frames):
                total += nn(at[b * frames + t], cotp[b, t + k])
            add_tap(0, k, total, b)
        if b == clips - 1:
            tm_copy(0).start()
        spread_own(d3, dm, True, b * frames, (b + 1) * frames)
        d_halo(b).wait()
        spread_halo(d3, dh, True, b * frames, (b + 1) * frames)
        if b < clips - 1:
            for i in range(3):
                spatial_grad(b, i)
            serve(2)

    last = clips - 1
    stage_x(0)
    spatial_grad(last, 0)
    tm_copy(1).start()
    spatial_grad(last, 1)
    tm_copy(2).start()
    stage_x(1)
    spatial_grad(last, 2)
    tm_copy(3).start()
    stage_x(2)
    stage_z(0)
    stage_x(3)
    serve(2)

    for b in range(clips):
        for t in range(1, frames):
            glat[b, t] = (back_sum(b, t) * mask_of(b, t)).astype(BF)
        if b == 0:
            stage_z(1)
            stage_g(0)
    stage_z(2)
    stage_g(1)
    stage_z(3)
    for b in range(clips):
        pre[b] = back_sum(b, 0)
    stage_xg(0)
    stage_g(2)
    stage_g(3)
    stage_xg(1)
    serve(len(hops))

    total = jnp.zeros((chans, chans), F32)
    for b in range(clips):
        ft[b] = fst[b].T
        for t in range(frames):
            total += nn(ft[b], cotp[b, t])
    add_tap(4, 0, total, 0)
    tm_copy(4).start()

    @pl.when(s == 0)
    def _():
        for b in range(clips):
            high = csum[b].astype(BF)
            low = (csum[b] - high.astype(F32)).astype(BF)
            pre[b] += nt(high, cw[...]) + nt(low, cw[...])

    for b in range(clips):
        glat[b, 0] = (pre[b] * mask_of(b, 0)).astype(BF)
    stage_x(4)
    stage_tg(0)
    stage_xg(2)

    for b in range(clips):
        cond = nn(fst[b], cw[...])
        for t in range(frames):
            bt = b * frames + t
            total = xm[bt].astype(F32) + cond
            for k in range(t + 1):
                total += nn(actp[b, frames + t - k], tw[k])
            pre[bt] = total
        if b == 0:
            stage_z(4)
    stage_xg(3)
    stage_tg(1)
    stage_g(4)
    for b in range(clips):
        @pl.when(s > 0)
        def _():
            act_copy(b).wait_recv()

        for t in range(frames):
            bt = b * frames + t
            total = pre[bt]
            for k in range(t + 1, 3):
                total += nn(actp[b, frames + t - k], tw[k])
            out[b, t] = (total * mask_of(b, t)).astype(BF)

    stage_tg(2)
    stage_xg(4)
    stage_tg(3)
    stage_tg(4)
    for k in range(5):
        stage_end(k)
    gtm[...] = res[0:3 * chans]
    gcd[...] = res[base[4]:base[4] + chans]
    for i in range(3):
        gsp[i * 3 * chans:(i + 1) * 3 * chans] = res[base[1 + i]:base[1 + i] + 3 * chans]

    for level in range(levels):
        for b in range(clips):
            first_done(level, b)
            sum_done(level, b)

    @pl.when(s > 0)
    def _():
        for b in range(clips):
            cot_copy(b).wait_send()

    @pl.when(s < n - 1)
    def _():
        for b in range(clips):
            act_copy(b).wait_send()

    for k in range(5):
        tm_copy(k).wait_send()
        x_copy(k).wait_send()
        for d in range(1, half):
            z_copy(k, d).wait_send()
            g_copy(k, d, q).wait_send()
        xg_copy(k, xb).wait_send()
        tg_copy(k, c).wait_send()


def on_device(latents, cotangent, valid_frames, spatial_weight, temporal_weight, cond_weight):
    clips, frames, rows, cols, chans = latents.shape
    n = lax.axis_size("space")
    slab = lax.axis_index("space")
    frame_ids = slab * frames + jnp.arange(frames, dtype=jnp.int32)
    mask = (frame_ids[None, :] < valid_frames[:, None]).astype(F32).reshape(clips * frames)
    scale = (clips * frames * rows * cols * n * lax.axis_size("tm")) ** (-0.5)
    pos = rows * cols
    unit = 32 * n
    sizes = [-(-taps * chans // unit) * unit for taps in (3, 3, 3, 3, 1)]
    total = sum(sizes)
    bt = clips * frames
    levels = len(bits_of(n))
    half = n // 2
    dma = pltpu.SemaphoreType.DMA
    big = (clips, frames, pos, chans)
    scratch = [
        pltpu.VMEM((bt, pos, chans), BF),
        pltpu.VMEM((bt, cols, chans), BF),
        pltpu.VMEM((bt, pos + 2 * cols, 3 * chans), BF),
        pltpu.VMEM((bt, chans, pos), BF),
        pltpu.VMEM((bt, pos, chans), F32),
        pltpu.VMEM((clips, 2 * frames, pos, chans), BF),
        pltpu.VMEM((bt, chans, pos), BF),
        pltpu.VMEM((clips, 2 * frames, pos, chans), BF),
        pltpu.VMEM((bt, pos, chans), BF),
        pltpu.VMEM((bt, cols, chans), BF),
        pltpu.VMEM((clips, pos, chans), BF),
        pltpu.VMEM((clips, chans, pos), BF),
        pltpu.VMEM((clips, pos, chans), F32),
        pltpu.VMEM((clips, pos, chans), BF),
        pltpu.VMEM((levels, clips, pos, chans), BF),
        pltpu.VMEM((clips, pos, chans), F32),
        pltpu.VMEM((total, chans), F32),
        pltpu.VMEM((total // 2, chans), F32),
        pltpu.VMEM((total // 4, chans), BF),
        pltpu.VMEM((total // 4, chans), BF),
        pltpu.VMEM((total // 4, chans), F32),
        pltpu.VMEM((total // 4, chans), BF),
        pltpu.VMEM((half - 1, total // (2 * n), chans), BF),
        pltpu.VMEM((total, chans), BF),
        dma((2, 1 + clips)), dma((2, clips)), dma((2, clips)),
        dma((2, levels, clips)), dma((2, levels, clips)),
        dma((2, 5)), dma((2, 5)), dma((5, half - 1)), dma((5, half - 1)),
        dma((5, half - 1)), dma((5, half - 1)), dma((2, 5)), dma((2, 5)),
    ]
    vmem = pl.BlockSpec(memory_space=pltpu.VMEM)
    smem = pl.BlockSpec(memory_space=pltpu.SMEM)
    shape = jax.ShapeDtypeStruct
    outs = pl.pallas_call(
        functools.partial(kernel, n, (clips, frames, rows, cols, chans, sizes), scale),
        out_shape=[
            shape(big, BF), shape(big, BF), shape((9 * chans, chans), BF),
            shape((3 * chans, chans), BF), shape((chans, chans), BF)],
        in_specs=[vmem, vmem, smem, vmem, vmem, vmem],
        out_specs=[vmem] * 5,
        scratch_shapes=scratch,
        compiler_params=pltpu.CompilerParams(
            collective_id=0, has_side_effects=True, vmem_limit_bytes=58 * 2**20),
    )(
        latents.reshape(big), cotangent.reshape(big), mask,
        spatial_weight.reshape(3, 3 * chans, chans), temporal_weight, cond_weight)
    output, grad_latents, grad_spatial, grad_temporal, grad_cond = outs
    return (
        output.reshape(latents.shape), grad_latents.reshape(latents.shape),
        grad_spatial.reshape(9, chans, chans), grad_temporal.reshape(3, chans, chans), grad_cond)


def solution(mesh):
    return jax.shard_map(
        on_device,
        mesh=mesh,
        in_specs=(
            P("groups", "space", "tm", None, None),
            P("groups", "space", "tm", None, None),
            P("groups"),
            P(),
            P(),
            P(),
        ),
        out_specs=(
            P("groups", "space", "tm", None, None),
            P("groups", "space", "tm", None, None),
            P("groups", None, None),
            P("groups", None, None),
            P("groups", None),
        ),
        check_vma=False,
    )
```

```python
import functools

import jax
import jax.numpy as jnp
from jax import lax
from jax.experimental import pallas as pl
from jax.experimental.pallas import tpu as pltpu
from jax.sharding import PartitionSpec as P

MESH = pl.DeviceIdType.MESH
BF = jnp.bfloat16
F32 = jnp.float32


def nn(left, right):
    return jnp.dot(left, right, preferred_element_type=F32)


def nt(left, right):
    return lax.dot_general(left, right, (((1,), (1,)), ((), ())), preferred_element_type=F32)


def bits_of(count):
    far = []
    bit = 2
    while bit < count:
        far.append(bit)
        bit *= 2
    return far + ([1] if count > 1 else [])


def kernel(n, dims, scale, *refs):
    clips, frames, rows, cols, chans, sizes = dims
    (lat, cotan, mask, sw, tw, cw, out, glat, gsp, gtm, gcd,
     xm, xh, x3, xt, pre, actp, at, cotp, dm, dh, fst, ft, csum, cs, cr, cb,
     acc, tmr, xs, xr, zs, zr, res, swt, twt,
     halo_sem, cot_sem, act_sem, first_sem, sum_sem, tm_sem, x_sem, z_send, z_recv,
     g_send, g_recv, tg_sem) = refs
    d3 = x3
    group = lax.axis_index("groups")
    s = lax.axis_index("space")
    c = lax.axis_index("tm")
    half = n // 2
    xb = lax.rem(s, 2)
    q = lax.div(s, 2)
    pos = rows * cols
    order = bits_of(n)
    levels = len(order)

    def at_dev(space, core):
        return (group, space, core)

    def copy(src, dst, sems, dev):
        return pltpu.make_async_remote_copy(
            src_ref=src, dst_ref=dst, send_sem=sems[0], recv_sem=sems[1],
            device_id=dev, device_id_type=MESH)

    def pair(sem, *index):
        return sem.at[(0,) + index], sem.at[(1,) + index]

    partner = at_dev(s, 1 - c)
    side = at_dev(s + 1 - 2 * xb, c)

    barrier = pltpu.get_barrier_semaphore()
    pl.semaphore_signal(barrier, inc=1, device_id=partner, device_id_type=MESH)
    for d in range(1, n):
        pl.semaphore_signal(
            barrier, inc=1, device_id=at_dev(lax.rem(s + d, n), c), device_id_type=MESH)
    pl.semaphore_wait(barrier, n)

    def mask_of(b, t):
        return mask[b * frames + t]

    for b in range(clips):
        for t in range(frames):
            cotp[b, t] = (cotan[b, t].astype(F32) * mask_of(b, t)).astype(BF)

    def cot_copy(b):
        return copy(cotp.at[b, pl.ds(0, frames)], cotp.at[b, pl.ds(frames, frames)],
                    pair(cot_sem, b), at_dev(jnp.maximum(s - 1, 0), c))

    def act_copy(b):
        return copy(actp.at[b, pl.ds(frames, frames)], actp.at[b, pl.ds(0, frames)],
                    pair(act_sem, b), at_dev(jnp.minimum(s + 1, n - 1), c))

    @pl.when(s > 0)
    def _():
        for b in range(clips):
            cot_copy(b).start()

    for b in range(clips):
        for t in range(frames):
            xm[b * frames + t] = (lat[b, t].astype(F32) * mask_of(b, t)).astype(BF)

    edge = pl.ds(pl.multiple_of((1 - c) * (rows - 1) * cols, cols), cols)
    x_halo = copy(xm.at[:, edge], xh, pair(halo_sem, 0), partner)
    x_halo.start()

    def d_halo(b):
        span = pl.ds(b * frames, frames)
        return copy(dm.at[span, edge], dh.at[span], pair(halo_sem, 1 + b), partner)

    def clear(upto):
        held = jnp.bool_(True)
        for bit in upto:
            held = held & (lax.rem(lax.div(s, bit), 2) == 0)
        return held

    def has(bit):
        return lax.rem(lax.div(s, bit), 2) == 1

    out_order = order[::-1]

    def first_copy(level, b):
        return copy(fst.at[b], fst.at[b], pair(first_sem, level, b),
                    at_dev(jnp.minimum(s + out_order[level], n - 1), c))

    def first_send(level, b):
        @pl.when(clear(out_order[level:]))
        def _():
            first_copy(level, b).start()

    def first_recv(level, b):
        @pl.when(has(out_order[level]) & clear(out_order[level + 1:]))
        def _():
            first_copy(level, b).wait_recv()

    def first_done(level, b):
        @pl.when(clear(out_order[level:]))
        def _():
            first_copy(level, b).wait_send()

    def sum_copy(level, b):
        return copy(cs.at[b], cr.at[level, b], pair(sum_sem, level, b),
                    at_dev(jnp.maximum(s - order[level], 0), c))

    def sum_send(level, b):
        @pl.when(has(order[level]) & clear(order[:level]))
        def _():
            cs[b] = csum[b].astype(BF)
            sum_copy(level, b).start()

    def sum_recv(level, b):
        @pl.when(clear(order[:level + 1]))
        def _():
            sum_copy(level, b).wait_recv()
            csum[b] += cr[level, b].astype(F32)

    def sum_done(level, b):
        @pl.when(has(order[level]) & clear(order[:level]))
        def _():
            sum_copy(level, b).wait_send()

    hops = sorted(((level, b) for level in range(levels) for b in range(clips)),
                  key=lambda hop: (hop[0] + hop[1], hop[0]))

    def serve(count):
        for _ in range(min(count, len(hops))):
            level, b = hops.pop(0)
            first_recv(level, b)
            sum_recv(level, b)
            if level + 1 < levels:
                first_send(level + 1, b)
                sum_send(level + 1, b)

    @pl.when(s == 0)
    def _():
        for b in range(clips):
            fst[b] = xm[b * frames]

    for b in range(clips):
        first_send(0, b)
        total = cotp[b, 0].astype(F32)
        for t in range(1, frames):
            total += cotp[b, t].astype(F32)
        csum[b] = total
        sum_send(0, b)

    @pl.when(s == n - 1)
    def _():
        cotp[:, frames:] = jnp.zeros((clips, frames, pos, chans), BF)

    @pl.when(s == 0)
    def _():
        actp[:, :frames] = jnp.zeros((clips, frames, pos, chans), BF)

    ids = lax.broadcasted_iota(jnp.int32, (cols, chans), 0)

    def spread(dst, bt, block, value, flip):
        wide = value.astype(F32)
        prev = jnp.where(ids == 0, 0.0, pltpu.roll(wide, 1, 0)).astype(BF)
        nxt = jnp.where(ids == cols - 1, 0.0, pltpu.roll(wide, cols - 1, 0)).astype(BF)
        span = pl.ds(pl.multiple_of(block * cols, cols), cols)
        lo, hi = (nxt, prev) if flip else (prev, nxt)
        dst[bt, span, 0:chans] = lo
        dst[bt, span, chans:2 * chans] = value
        dst[bt, span, 2 * chans:3 * chans] = hi

    def spread_own(dst, src, flip, begin, end):
        @pl.loop(begin, end)
        def _(bt):
            for r in range(rows):
                spread(dst, bt, r + 1, src[bt, r * cols:(r + 1) * cols], flip)

    def spread_halo(dst, src, flip, begin, end):
        @pl.loop(begin, end)
        def _(bt):
            got = src[bt].astype(F32)
            spread(dst, bt, 0, (got * c.astype(F32)).astype(BF), flip)
            spread(dst, bt, rows + 1, (got * (1 - c).astype(F32)).astype(BF), flip)

    spread_own(x3, xm, False, 0, clips * frames)

    @pl.loop(0, clips * frames)
    def _(bt):
        xt[bt] = xm[bt].T

    x_halo.wait()
    spread_halo(x3, xh, False, 0, clips * frames)

    for b in range(clips):
        @pl.loop(0, frames)
        def _(t):
            bt = b * frames + t
            total = nn(x3[bt, 0:pos], sw[0])
            for i in range(1, 3):
                total += nn(x3[bt, i * cols:i * cols + pos], sw[i])
            pre[bt] = total
            act = (total * jax.nn.sigmoid(total)).astype(BF)
            actp[b, frames + t] = act
            at[bt] = act.T

    serve(1)

    for k in range(3):
        twt[k] = tw[k].T
        for j in range(3):
            span = slice(j * chans, (j + 1) * chans)
            swt[k, span] = sw[k, span].T

    base = [sum(sizes[:k]) for k in range(len(sizes))]

    def rows_at(start, size):
        return pl.ds(pl.multiple_of(start, 16), size)

    def tm_copy(k):
        size = sizes[k] // 2
        src = acc.at[rows_at(base[k] + (1 - c) * size, size)]
        return copy(src, tmr.at[pl.ds(base[k] // 2, size)], pair(tm_sem, k), partner)

    def z_peer(d):
        other = lax.rem(q + d, half)
        return other, at_dev(2 * other + xb, c)

    def z_copy(k, d):
        size = sizes[k] // n
        other, dev = z_peer(d)
        src = zs.at[rows_at(base[k] // 2 + other * size, size)]
        dst = zr.at[d - 1, pl.ds(base[k] // n, size)]
        return copy(src, dst, (z_send.at[k, d - 1], z_recv.at[k, d - 1]), dev)

    def x_copy(k):
        span = pl.ds(base[k] // n, sizes[k] // n)
        return copy(xs.at[span], xr.at[span], pair(x_sem, k), side)

    def g_copy(k, d, place):
        size = sizes[k] // n
        own = res.at[rows_at(base[k] + c * (sizes[k] // 2) + place * size, size)]
        return copy(own, own, (g_send.at[k, d - 1], g_recv.at[k, d - 1]), z_peer(d)[1])

    def tg_copy(k, bit):
        size = sizes[k] // 2
        own = res.at[rows_at(base[k] + bit * size, size)]
        return copy(own, own, pair(tg_sem, k), partner)

    def stage_z(k):
        tm_copy(k).wait_recv()
        size = sizes[k] // 2
        span = pl.ds(base[k] // 2, size)
        total = acc[rows_at(base[k] + c * size, size)] + tmr[span]
        tmr[span] = total
        zs[span] = total.astype(BF)
        for d in range(1, half):
            z_copy(k, d).start()

    def stage_x(k):
        size = sizes[k] // n
        span = pl.ds(base[k] // n, size)
        total = tmr[rows_at(base[k] // 2 + q * size, size)]
        for d in range(1, half):
            z_copy(k, d).wait_recv()
            total += zr[d - 1, span].astype(F32)
        xs[span] = total.astype(BF)
        x_copy(k).start()

    def stage_g(k):
        size = sizes[k] // n
        span = pl.ds(base[k] // n, size)
        x_copy(k).wait_recv()
        total = xs[span].astype(F32) + xr[span].astype(F32)
        res[rows_at(base[k] + c * (sizes[k] // 2) + q * size, size)] = (total * scale).astype(BF)
        for d in range(1, half):
            g_copy(k, d, q).start()

    def stage_tg(k):
        for d in range(1, half):
            g_copy(k, d, lax.rem(q + half - d, half)).wait_recv()
        tg_copy(k, c).start()

    def stage_end(k):
        tg_copy(k, 1 - c).wait_recv()

    def add_tap(k, tap, value, b):
        span = slice(base[k] + tap * chans, base[k] + (tap + 1) * chans)
        if b == 0:
            acc[span] = value
        else:
            acc[span] += value

    for k, taps in enumerate((3, 3, 3, 3, 1)):
        if sizes[k] > taps * chans:
            acc[base[k] + taps * chans:base[k] + sizes[k]] = jnp.zeros(
                (sizes[k] - taps * chans, chans), F32)

    def spatial_grad(b, i):
        for j in range(3):
            total = jnp.zeros((chans, chans), F32)
            for bt in range(b * frames, (b + 1) * frames):
                piece = d3[bt, (2 - i) * cols:(2 - i) * cols + pos, j * chans:(j + 1) * chans]
                total += nn(xt[bt], piece)
            add_tap(1 + i, j, total, b)

    def back_sum(b, t):
        bt = b * frames + t
        total = cotp[b, t].astype(F32)
        for i in range(3):
            total += nn(d3[bt, (2 - i) * cols:(2 - i) * cols + pos], swt[i])
        return total

    for b in range(clips):
        @pl.when(s < n - 1)
        def _():
            cot_copy(b).wait_recv()

        if b == 0:
            serve(2)
        if b == clips - 1:
            @pl.when(s < n - 1)
            def _():
                for each in range(clips):
                    act_copy(each).start()

        @pl.loop(0, frames)
        def _(t):
            bt = b * frames + t
            dact = nn(cotp[b, t], twt[0])
            for k in range(1, 3):
                dact += nn(cotp[b, t + k], twt[k])
            value = pre[bt]
            sig = jax.nn.sigmoid(value)
            dm[bt] = (dact * sig * (1.0 + value * (1.0 - sig))).astype(BF)

        d_halo(b).start()
        for k in range(3):
            total = jnp.zeros((chans, chans), F32)
            for t in range(frames):
                total += nn(at[b * frames + t], cotp[b, t + k])
            add_tap(0, k, total, b)
        if b == clips - 1:
            tm_copy(0).start()
        spread_own(d3, dm, True, b * frames, (b + 1) * frames)
        d_halo(b).wait()
        spread_halo(d3, dh, True, b * frames, (b + 1) * frames)
        if b < clips - 1:
            for i in range(3):
                spatial_grad(b, i)
            serve(2)

    last = clips - 1
    stage_z(0)
    spatial_grad(last, 0)
    tm_copy(1).start()
    spatial_grad(last, 1)
    tm_copy(2).start()
    stage_z(1)
    spatial_grad(last, 2)
    tm_copy(3).start()
    stage_z(2)
    stage_x(0)
    stage_z(3)
    serve(len(hops))

    total = jnp.zeros((chans, chans), F32)
    for b in range(clips):
        ft[b] = fst[b].T
        for t in range(frames):
            total += nn(ft[b], cotp[b, t])
    add_tap(4, 0, total, 0)
    tm_copy(4).start()

    @pl.when(s == 0)
    def _():
        for b in range(clips):
            high = csum[b].astype(BF)
            low = (csum[b] - high.astype(F32)).astype(BF)
            cb[b] = nt(high, cw[...]) + nt(low, cw[...])

    @pl.when(s > 0)
    def _():
        cb[...] = jnp.zeros((clips, pos, chans), F32)

    stage_x(1)
    stage_z(4)
    for b in range(clips):
        for t in range(frames):
            total = back_sum(b, t)
            if t == 0:
                total += cb[b]
            glat[b, t] = (total * mask_of(b, t)).astype(BF)
        if b == 0:
            stage_x(2)
            stage_g(0)
    stage_x(3)
    stage_g(1)
    stage_x(4)

    for b in range(clips):
        cond = nn(fst[b], cw[...])
        for t in range(frames):
            bt = b * frames + t
            total = xm[bt].astype(F32) + cond
            for k in range(t + 1):
                total += nn(actp[b, frames + t - k], tw[k])
            pre[bt] = total
    stage_g(2)
    stage_g(3)
    stage_tg(0)
    stage_g(4)
    for b in range(clips):
        @pl.when(s > 0)
        def _():
            act_copy(b).wait_recv()

        for t in range(frames):
            bt = b * frames + t
            total = pre[bt]
            for k in range(t + 1, 3):
                total += nn(actp[b, frames + t - k], tw[k])
            out[b, t] = (total * mask_of(b, t)).astype(BF)

    for k in range(1, 5):
        stage_tg(k)
    for k in range(5):
        stage_end(k)
    gtm[...] = res[0:3 * chans]
    gcd[...] = res[base[4]:base[4] + chans]
    for i in range(3):
        gsp[i * 3 * chans:(i + 1) * 3 * chans] = res[base[1 + i]:base[1 + i] + 3 * chans]

    for level in range(levels):
        for b in range(clips):
            first_done(level, b)
            sum_done(level, b)

    @pl.when(s > 0)
    def _():
        for b in range(clips):
            cot_copy(b).wait_send()

    @pl.when(s < n - 1)
    def _():
        for b in range(clips):
            act_copy(b).wait_send()

    for k in range(5):
        tm_copy(k).wait_send()
        x_copy(k).wait_send()
        for d in range(1, half):
            z_copy(k, d).wait_send()
            g_copy(k, d, q).wait_send()
        tg_copy(k, c).wait_send()


def hand_over(*refs):
    sems = refs[10]
    copies = [pltpu.make_async_copy(refs[i], refs[5 + i], sems.at[i]) for i in range(5)]
    for each in copies:
        each.start()
    for each in copies:
        each.wait()


def on_device(latents, cotangent, valid_frames, spatial_weight, temporal_weight, cond_weight):
    clips, frames, rows, cols, chans = latents.shape
    n = lax.axis_size("space")
    slab = lax.axis_index("space")
    frame_ids = slab * frames + jnp.arange(frames, dtype=jnp.int32)
    mask = (frame_ids[None, :] < valid_frames[:, None]).astype(F32).reshape(clips * frames)
    scale = (clips * frames * rows * cols * n * lax.axis_size("tm")) ** (-0.5)
    pos = rows * cols
    unit = 16 * n
    sizes = [-(-taps * chans // unit) * unit for taps in (3, 3, 3, 3, 1)]
    total = sum(sizes)
    bt = clips * frames
    levels = len(bits_of(n))
    half = n // 2
    dma = pltpu.SemaphoreType.DMA
    big = (clips, frames, pos, chans)
    scratch = [
        pltpu.VMEM((bt, pos, chans), BF),
        pltpu.VMEM((bt, cols, chans), BF),
        pltpu.VMEM((bt, pos + 2 * cols, 3 * chans), BF),
        pltpu.VMEM((bt, chans, pos), BF),
        pltpu.VMEM((bt, pos, chans), F32),
        pltpu.VMEM((clips, 2 * frames, pos, chans), BF),
        pltpu.VMEM((bt, chans, pos), BF),
        pltpu.VMEM((clips, 2 * frames, pos, chans), BF),
        pltpu.VMEM((bt, pos, chans), BF),
        pltpu.VMEM((bt, cols, chans), BF),
        pltpu.VMEM((clips, pos, chans), BF),
        pltpu.VMEM((clips, chans, pos), BF),
        pltpu.VMEM((clips, pos, chans), F32),
        pltpu.VMEM((clips, pos, chans), BF),
        pltpu.VMEM((levels, clips, pos, chans), BF),
        pltpu.VMEM((clips, pos, chans), F32),
        pltpu.VMEM((total, chans), F32),
        pltpu.VMEM((total // 2, chans), F32),
        pltpu.VMEM((total // n, chans), BF),
        pltpu.VMEM((total // n, chans), BF),
        pltpu.VMEM((total // 2, chans), BF),
        pltpu.VMEM((half - 1, total // n, chans), BF),
        pltpu.VMEM((total, chans), BF),
        pltpu.VMEM((3, 3 * chans, chans), BF),
        pltpu.VMEM((3, chans, chans), BF),
        dma((2, 1 + clips)), dma((2, clips)), dma((2, clips)),
        dma((2, levels, clips)), dma((2, levels, clips)),
        dma((2, 5)), dma((2, 5)), dma((5, half - 1)), dma((5, half - 1)),
        dma((5, half - 1)), dma((5, half - 1)), dma((2, 5)),
    ]
    vmem = pl.BlockSpec(memory_space=pltpu.VMEM)
    smem = pl.BlockSpec(memory_space=pltpu.SMEM)
    shape = jax.ShapeDtypeStruct
    outs = pl.pallas_call(
        functools.partial(kernel, n, (clips, frames, rows, cols, chans, sizes), scale),
        out_shape=[
            shape(big, BF), shape(big, BF), shape((9 * chans, chans), BF),
            shape((3 * chans, chans), BF), shape((chans, chans), BF)],
        in_specs=[vmem, vmem, smem, vmem, vmem, vmem],
        out_specs=[vmem] * 5,
        scratch_shapes=scratch,
        compiler_params=pltpu.CompilerParams(
            collective_id=0, has_side_effects=True, vmem_limit_bytes=58 * 2**20),
    )(
        latents.reshape(big), cotangent.reshape(big), mask,
        spatial_weight.reshape(3, 3 * chans, chans), temporal_weight, cond_weight)
    anywhere = pl.BlockSpec(memory_space=pl.ANY)
    outs = pl.pallas_call(
        hand_over,
        out_shape=[shape(one.shape, one.dtype) for one in outs],
        in_specs=[anywhere] * 5,
        out_specs=[anywhere] * 5,
        scratch_shapes=[dma((5,))],
    )(*outs)
    output, grad_latents, grad_spatial, grad_temporal, grad_cond = outs
    return (
        output.reshape(latents.shape), grad_latents.reshape(latents.shape),
        grad_spatial.reshape(9, chans, chans), grad_temporal.reshape(3, chans, chans), grad_cond)


def solution(mesh):
    return jax.shard_map(
        on_device,
        mesh=mesh,
        in_specs=(
            P("groups", "space", "tm", None, None),
            P("groups", "space", "tm", None, None),
            P("groups"),
            P(),
            P(),
            P(),
        ),
        out_specs=(
            P("groups", "space", "tm", None, None),
            P("groups", "space", "tm", None, None),
            P("groups", None, None),
            P("groups", None, None),
            P("groups", None),
        ),
        check_vma=False,
    )
```

```python
import functools

import jax
import jax.numpy as jnp
from jax import lax
from jax.experimental import pallas as pl
from jax.experimental.pallas import tpu as pltpu
from jax.sharding import PartitionSpec as P

MESH = pl.DeviceIdType.MESH
BF = jnp.bfloat16
F32 = jnp.float32


def nn(left, right):
    return jnp.dot(left, right, preferred_element_type=F32)


def nt(left, right):
    return lax.dot_general(left, right, (((1,), (1,)), ((), ())), preferred_element_type=F32)


def bits_of(count):
    far = []
    bit = 2
    while bit < count:
        far.append(bit)
        bit *= 2
    return far + ([1] if count > 1 else [])


def kernel(n, dims, scale, *refs):
    clips, frames, rows, cols, chans, sizes = dims
    (lat, cotan, mask, sw, tw, cw, out, glat, gsp, gtm, gcd,
     xm, xh, x3, xt, pre, actp, at, cotp, dm, dh, fst, ft, csum, cs, cr, cb,
     acc, tmr, xs, xr, zs, zr, res, swt, twt,
     halo_sem, cot_sem, act_sem, first_sem, sum_sem, tm_sem, x_sem, z_sem,
     g_sem, tg_sem) = refs
    d3 = x3
    group = lax.axis_index("groups")
    s = lax.axis_index("space")
    c = lax.axis_index("tm")
    half = n // 2
    xb = lax.rem(s, 2)
    q = lax.div(s, 2)
    pos = rows * cols
    order = bits_of(n)
    levels = len(order)

    def at_dev(space, core):
        return (group, space, core)

    def copy(src, dst, sems, dev):
        return pltpu.make_async_remote_copy(
            src_ref=src, dst_ref=dst, send_sem=sems[0], recv_sem=sems[1],
            device_id=dev, device_id_type=MESH)

    def pair(sem, *index):
        return sem.at[(0,) + index], sem.at[(1,) + index]

    partner = at_dev(s, 1 - c)
    side = at_dev(s + 1 - 2 * xb, c)

    barrier = pltpu.get_barrier_semaphore()
    pl.semaphore_signal(barrier, inc=1, device_id=partner, device_id_type=MESH)
    for d in range(1, n):
        pl.semaphore_signal(
            barrier, inc=1, device_id=at_dev(lax.rem(s + d, n), c), device_id_type=MESH)
    pl.semaphore_wait(barrier, n)

    def mask_of(b, t):
        return mask[b * frames + t]

    for b in range(clips):
        for t in range(frames):
            cotp[b, t] = (cotan[b, t].astype(F32) * mask_of(b, t)).astype(BF)

    def cot_copy(b):
        return copy(cotp.at[b, pl.ds(0, frames)], cotp.at[b, pl.ds(frames, frames)],
                    pair(cot_sem, b), at_dev(jnp.maximum(s - 1, 0), c))

    def act_copy(b):
        return copy(actp.at[b, pl.ds(frames, frames)], actp.at[b, pl.ds(0, frames)],
                    pair(act_sem, b), at_dev(jnp.minimum(s + 1, n - 1), c))

    @pl.when(s > 0)
    def _():
        for b in range(clips):
            cot_copy(b).start()

    for b in range(clips):
        for t in range(frames):
            xm[b * frames + t] = (lat[b, t].astype(F32) * mask_of(b, t)).astype(BF)

    edge = pl.ds(pl.multiple_of((1 - c) * (rows - 1) * cols, cols), cols)
    x_halo = copy(xm.at[:, edge], xh, pair(halo_sem, 0), partner)
    x_halo.start()

    def d_halo(b):
        span = pl.ds(b * frames, frames)
        return copy(dm.at[span, edge], dh.at[span], pair(halo_sem, 1 + b), partner)

    def clear(upto):
        held = jnp.bool_(True)
        for bit in upto:
            held = held & (lax.rem(lax.div(s, bit), 2) == 0)
        return held

    def has(bit):
        return lax.rem(lax.div(s, bit), 2) == 1

    out_order = order[::-1]

    def first_copy(level, b):
        return copy(fst.at[b], fst.at[b], pair(first_sem, level, b),
                    at_dev(jnp.minimum(s + out_order[level], n - 1), c))

    def first_send(level, b):
        @pl.when(clear(out_order[level:]))
        def _():
            first_copy(level, b).start()

    def first_recv(level, b):
        @pl.when(has(out_order[level]) & clear(out_order[level + 1:]))
        def _():
            first_copy(level, b).wait_recv()

    def first_done(level, b):
        @pl.when(clear(out_order[level:]))
        def _():
            first_copy(level, b).wait_send()

    def sum_copy(level, b):
        return copy(cs.at[b], cr.at[level, b], pair(sum_sem, level, b),
                    at_dev(jnp.maximum(s - order[level], 0), c))

    def sum_send(level, b):
        @pl.when(has(order[level]) & clear(order[:level]))
        def _():
            cs[b] = csum[b].astype(BF)
            sum_copy(level, b).start()

    def sum_recv(level, b):
        @pl.when(clear(order[:level + 1]))
        def _():
            sum_copy(level, b).wait_recv()
            csum[b] += cr[level, b].astype(F32)

    def sum_done(level, b):
        @pl.when(has(order[level]) & clear(order[:level]))
        def _():
            sum_copy(level, b).wait_send()

    hops = sorted(((level, b) for level in range(levels) for b in range(clips)),
                  key=lambda hop: (hop[0] + hop[1], hop[0]))

    def serve(count):
        for _ in range(min(count, len(hops))):
            level, b = hops.pop(0)
            first_recv(level, b)
            if level + 1 < levels:
                first_send(level + 1, b)

    def serve_sum(level):
        for b in range(clips):
            sum_recv(level, b)
            if level + 1 < levels:
                sum_send(level + 1, b)

    @pl.when(s == 0)
    def _():
        for b in range(clips):
            fst[b] = xm[b * frames]

    for b in range(clips):
        first_send(0, b)
        total = cotp[b, 0].astype(F32)
        for t in range(1, frames):
            total += cotp[b, t].astype(F32)
        csum[b] = total

    @pl.when(s == n - 1)
    def _():
        cotp[:, frames:] = jnp.zeros((clips, frames, pos, chans), BF)

    @pl.when(s == 0)
    def _():
        actp[:, :frames] = jnp.zeros((clips, frames, pos, chans), BF)

    ids = lax.broadcasted_iota(jnp.int32, (cols, chans), 0)

    def spread(dst, bt, block, value, flip):
        wide = value.astype(F32)
        prev = jnp.where(ids == 0, 0.0, pltpu.roll(wide, 1, 0)).astype(BF)
        nxt = jnp.where(ids == cols - 1, 0.0, pltpu.roll(wide, cols - 1, 0)).astype(BF)
        span = pl.ds(pl.multiple_of(block * cols, cols), cols)
        lo, hi = (nxt, prev) if flip else (prev, nxt)
        dst[bt, span, 0:chans] = lo
        dst[bt, span, chans:2 * chans] = value
        dst[bt, span, 2 * chans:3 * chans] = hi

    def spread_own(dst, src, flip, begin, end):
        @pl.loop(begin, end)
        def _(bt):
            for r in range(rows):
                spread(dst, bt, r + 1, src[bt, r * cols:(r + 1) * cols], flip)

    def spread_halo(dst, src, flip, begin, end):
        @pl.loop(begin, end)
        def _(bt):
            got = src[bt].astype(F32)
            spread(dst, bt, 0, (got * c.astype(F32)).astype(BF), flip)
            spread(dst, bt, rows + 1, (got * (1 - c).astype(F32)).astype(BF), flip)

    spread_own(x3, xm, False, 0, clips * frames)

    @pl.loop(0, clips * frames)
    def _(bt):
        xt[bt] = xm[bt].T

    x_halo.wait()
    spread_halo(x3, xh, False, 0, clips * frames)

    for b in range(clips):
        @pl.loop(0, frames)
        def _(t):
            bt = b * frames + t
            total = nn(x3[bt, 0:pos], sw[0])
            for i in range(1, 3):
                total += nn(x3[bt, i * cols:i * cols + pos], sw[i])
            pre[bt] = total
            act = (total * jax.nn.sigmoid(total)).astype(BF)
            actp[b, frames + t] = act
            at[bt] = act.T

    serve(1)

    for k in range(3):
        twt[k] = tw[k].T
        for j in range(3):
            span = slice(j * chans, (j + 1) * chans)
            swt[k, span] = sw[k, span].T

    base = [sum(sizes[:k]) for k in range(len(sizes))]

    def rows_at(start, size):
        return pl.ds(pl.multiple_of(start, 16), size)

    def tm_copy(k):
        size = sizes[k] // 2
        src = acc.at[rows_at(base[k] + (1 - c) * size, size)]
        return copy(src, tmr.at[pl.ds(base[k] // 2, size)], pair(tm_sem, k), partner)

    zbits = []
    while (1 << len(zbits)) < half:
        zbits.append(1 << len(zbits))

    def z_side(level):
        return lax.rem(lax.div(q, zbits[level]), 2)

    def z_dev(level):
        return at_dev(s + 2 * zbits[level] * (1 - 2 * z_side(level)), c)

    def kept(k, level):
        offset = 0
        for done in range(level):
            offset = offset + z_side(done) * (sizes[k] >> (done + 2))
        return offset

    def z_span(k, level):
        size = sizes[k] >> (level + 2)
        return pl.ds(base[k] // 2 + sizes[k] // 2 - 2 * size, size)

    def z_copy(k, level):
        span = z_span(k, level)
        return copy(zs.at[span], zr.at[span], pair(z_sem, k, level), z_dev(level))

    def x_copy(k):
        span = pl.ds(base[k] // n, sizes[k] // n)
        return copy(xs.at[span], xr.at[span], pair(x_sem, k), side)

    def g_copy(k, level, mine):
        size = sizes[k] >> (level + 2)
        which = z_side(level) if mine else 1 - z_side(level)
        start = base[k] + c * (sizes[k] // 2) + kept(k, level) + which * size
        own = res.at[rows_at(start, size)]
        return copy(own, own, pair(g_sem, k, level), z_dev(level))

    def tg_copy(k, bit):
        size = sizes[k] // 2
        own = res.at[rows_at(base[k] + bit * size, size)]
        return copy(own, own, pair(tg_sem, k), partner)

    def z_send(k, level):
        size = sizes[k] >> (level + 2)
        away = base[k] // 2 + kept(k, level) + (1 - z_side(level)) * size
        zs[z_span(k, level)] = tmr[rows_at(away, size)].astype(BF)
        z_copy(k, level).start()

    def stage_z(k):
        tm_copy(k).wait_recv()
        size = sizes[k] // 2
        span = pl.ds(base[k] // 2, size)
        tmr[span] += acc[rows_at(base[k] + c * size, size)]
        z_send(k, 0)

    def stage_zz(k, level):
        z_copy(k, level - 1).wait_recv()
        size = sizes[k] >> (level + 1)
        span = rows_at(base[k] // 2 + kept(k, level), size)
        tmr[span] += zr[z_span(k, level - 1)].astype(F32)
        if level < len(zbits):
            z_send(k, level)
        else:
            xs[pl.ds(base[k] // n, size)] = tmr[span].astype(BF)
            x_copy(k).start()

    def stage_g(k):
        size = sizes[k] // n
        span = pl.ds(base[k] // n, size)
        x_copy(k).wait_recv()
        total = xs[span].astype(F32) + xr[span].astype(F32)
        start = base[k] + c * (sizes[k] // 2) + kept(k, len(zbits))
        res[rows_at(start, size)] = (total * scale).astype(BF)
        g_copy(k, len(zbits) - 1, True).start()

    def stage_gg(k, level):
        g_copy(k, level, False).wait_recv()
        if level > 0:
            g_copy(k, level - 1, True).start()
        else:
            tg_copy(k, c).start()

    def stage_end(k):
        tg_copy(k, 1 - c).wait_recv()

    for k, taps in enumerate((3, 3, 3, 3, 1)):
        if sizes[k] > taps * chans:
            acc[base[k] + taps * chans:base[k] + sizes[k]] = jnp.zeros(
                (sizes[k] - taps * chans, chans), F32)

    def spatial_grad(b, i):
        @pl.loop(0, 3)
        def _(j):
            total = jnp.zeros((chans, chans), F32)
            for bt in range(b * frames, (b + 1) * frames):
                piece = d3[bt, (2 - i) * cols:(2 - i) * cols + pos,
                           pl.ds(pl.multiple_of(j * chans, chans), chans)]
                total += nn(xt[bt], piece)
            span = pl.ds(pl.multiple_of(base[1 + i] + j * chans, chans), chans)
            if b == 0:
                acc[span] = total
            else:
                acc[span] += total

    def back_sum(b, t):
        bt = b * frames + t
        total = cotp[b, t].astype(F32)
        for i in range(3):
            total += nn(d3[bt, (2 - i) * cols:(2 - i) * cols + pos], swt[i])
        return total

    for b in range(clips):
        @pl.when(s < n - 1)
        def _():
            cot_copy(b).wait_recv()

        if b == clips - 1:
            @pl.when(s < n - 1)
            def _():
                for each in range(clips):
                    act_copy(each).start()

            for each in range(clips):
                sum_send(0, each)

        @pl.loop(0, frames)
        def _(t):
            bt = b * frames + t
            dact = nn(cotp[b, t], twt[0])
            for k in range(1, 3):
                dact += nn(cotp[b, t + k], twt[k])
            value = pre[bt]
            sig = jax.nn.sigmoid(value)
            dm[bt] = (dact * sig * (1.0 + value * (1.0 - sig))).astype(BF)

        d_halo(b).start()

        @pl.loop(0, 3)
        def _(k):
            total = jnp.zeros((chans, chans), F32)
            for t in range(frames):
                total += nn(at[b * frames + t], cotp[b, t + k])
            span = pl.ds(pl.multiple_of(k * chans, chans), chans)
            if b == 0:
                acc[span] = total
            else:
                acc[span] += total

        if b == clips - 1:
            tm_copy(0).start()
        spread_own(d3, dm, True, b * frames, (b + 1) * frames)
        d_halo(b).wait()
        spread_halo(d3, dh, True, b * frames, (b + 1) * frames)
        if b < clips - 1:
            for i in range(3):
                spatial_grad(b, i)
            serve(2)

    last = clips - 1
    deep = len(zbits)

    def middle(k):
        for level in range(1, deep):
            stage_zz(k, level)

    def outer_gather(k):
        for level in range(deep - 1, 0, -1):
            stage_gg(k, level)

    stage_z(0)
    spatial_grad(last, 0)
    tm_copy(1).start()
    serve(2)
    spatial_grad(last, 1)
    tm_copy(2).start()
    stage_z(1)
    spatial_grad(last, 2)
    tm_copy(3).start()
    stage_z(2)
    middle(0)
    stage_z(3)
    serve(len(hops))

    total = jnp.zeros((chans, chans), F32)
    for b in range(clips):
        ft[b] = fst[b].T
        for t in range(frames):
            total += nn(ft[b], cotp[b, t])
    acc[base[4]:base[4] + chans] = total
    tm_copy(4).start()
    middle(1)
    stage_zz(0, deep)
    stage_z(4)

    @pl.loop(0, clips)
    def _(b):
        for t in range(1, frames):
            glat[b, t] = (back_sum(b, t) * mask_of(b, t)).astype(BF)

    middle(2)
    stage_zz(1, deep)
    stage_g(0)
    middle(3)
    serve_sum(0)

    @pl.loop(0, clips)
    def _(b):
        cb[b] = back_sum(b, 0)

    stage_zz(2, deep)
    stage_g(1)
    stage_zz(3, deep)
    outer_gather(0)
    middle(4)

    @pl.loop(0, clips)
    def _(b):
        cond = nn(fst[b], cw[...])
        for t in range(frames):
            bt = b * frames + t
            total = xm[bt].astype(F32) + cond
            for k in range(t + 1):
                total += nn(actp[b, frames + t - k], tw[k])
            pre[bt] = total

    stage_g(2)
    stage_zz(4, deep)
    stage_gg(0, 0)
    outer_gather(1)
    stage_g(3)
    for level in range(1, levels):
        serve_sum(level)
    stage_g(4)
    outer_gather(2)

    @pl.when(s == 0)
    def _():
        @pl.loop(0, clips)
        def _(b):
            high = csum[b].astype(BF)
            low = (csum[b] - high.astype(F32)).astype(BF)
            cb[b] += nt(high, cw[...]) + nt(low, cw[...])

    for b in range(clips):
        glat[b, 0] = (cb[b] * mask_of(b, 0)).astype(BF)
    stage_gg(1, 0)
    outer_gather(3)
    outer_gather(4)

    for b in range(clips):
        @pl.when(s > 0)
        def _():
            act_copy(b).wait_recv()

    @pl.loop(0, clips)
    def _(b):
        for t in range(frames):
            bt = b * frames + t
            total = pre[bt]
            for k in range(t + 1, 3):
                total += nn(actp[b, frames + t - k], tw[k])
            out[b, t] = (total * mask_of(b, t)).astype(BF)

    for k in range(2, 5):
        stage_gg(k, 0)
    for k in range(5):
        stage_end(k)
    gtm[...] = res[0:3 * chans]
    gcd[...] = res[base[4]:base[4] + chans]
    for i in range(3):
        gsp[i * 3 * chans:(i + 1) * 3 * chans] = res[base[1 + i]:base[1 + i] + 3 * chans]

    for level in range(levels):
        for b in range(clips):
            first_done(level, b)
            sum_done(level, b)

    @pl.when(s > 0)
    def _():
        for b in range(clips):
            cot_copy(b).wait_send()

    @pl.when(s < n - 1)
    def _():
        for b in range(clips):
            act_copy(b).wait_send()

    for k in range(5):
        tm_copy(k).wait_send()
        x_copy(k).wait_send()
        for level in range(len(zbits)):
            z_copy(k, level).wait_send()
            g_copy(k, level, True).wait_send()
        tg_copy(k, c).wait_send()


def hand_over(*refs):
    for i in range(5):
        refs[5 + i][...] = refs[i][...]


def on_device(latents, cotangent, valid_frames, spatial_weight, temporal_weight, cond_weight):
    clips, frames, rows, cols, chans = latents.shape
    n = lax.axis_size("space")
    slab = lax.axis_index("space")
    frame_ids = slab * frames + jnp.arange(frames, dtype=jnp.int32)
    mask = (frame_ids[None, :] < valid_frames[:, None]).astype(F32).reshape(clips * frames)
    scale = (clips * frames * rows * cols * n * lax.axis_size("tm")) ** (-0.5)
    pos = rows * cols
    unit = 16 * n
    sizes = [-(-taps * chans // unit) * unit for taps in (3, 3, 3, 3, 1)]
    total = sum(sizes)
    bt = clips * frames
    levels = len(bits_of(n))
    dma = pltpu.SemaphoreType.DMA
    big = (clips, frames, pos, chans)
    scratch = [
        pltpu.VMEM((bt, pos, chans), BF),
        pltpu.VMEM((bt, cols, chans), BF),
        pltpu.VMEM((bt, pos + 2 * cols, 3 * chans), BF),
        pltpu.VMEM((bt, chans, pos), BF),
        pltpu.VMEM((bt, pos, chans), F32),
        pltpu.VMEM((clips, 2 * frames, pos, chans), BF),
        pltpu.VMEM((bt, chans, pos), BF),
        pltpu.VMEM((clips, 2 * frames, pos, chans), BF),
        pltpu.VMEM((bt, pos, chans), BF),
        pltpu.VMEM((bt, cols, chans), BF),
        pltpu.VMEM((clips, pos, chans), BF),
        pltpu.VMEM((clips, chans, pos), BF),
        pltpu.VMEM((clips, pos, chans), F32),
        pltpu.VMEM((clips, pos, chans), BF),
        pltpu.VMEM((levels, clips, pos, chans), BF),
        pltpu.VMEM((clips, pos, chans), F32),
        pltpu.VMEM((total, chans), F32),
        pltpu.VMEM((total // 2, chans), F32),
        pltpu.VMEM((total // n, chans), BF),
        pltpu.VMEM((total // n, chans), BF),
        pltpu.VMEM((total // 2, chans), BF),
        pltpu.VMEM((total // 2, chans), BF),
        pltpu.VMEM((total, chans), BF),
        pltpu.VMEM((3, 3 * chans, chans), BF),
        pltpu.VMEM((3, chans, chans), BF),
        dma((2, 1 + clips)), dma((2, clips)), dma((2, clips)),
        dma((2, levels, clips)), dma((2, levels, clips)),
        dma((2, 5)), dma((2, 5)), dma((2, 5, levels)), dma((2, 5, levels)), dma((2, 5)),
    ]
    vmem = pl.BlockSpec(memory_space=pltpu.VMEM)
    smem = pl.BlockSpec(memory_space=pltpu.SMEM)
    shape = jax.ShapeDtypeStruct
    outs = pl.pallas_call(
        functools.partial(kernel, n, (clips, frames, rows, cols, chans, sizes), scale),
        out_shape=[
            shape(big, BF), shape(big, BF), shape((9 * chans, chans), BF),
            shape((3 * chans, chans), BF), shape((chans, chans), BF)],
        in_specs=[vmem, vmem, smem, vmem, vmem, vmem],
        out_specs=[vmem] * 5,
        scratch_shapes=scratch,
        compiler_params=pltpu.CompilerParams(
            collective_id=0, has_side_effects=True, vmem_limit_bytes=58 * 2**20),
    )(
        latents.reshape(big), cotangent.reshape(big), mask,
        spatial_weight.reshape(3, 3 * chans, chans), temporal_weight, cond_weight)
    outs = pl.pallas_call(
        hand_over,
        out_shape=[shape(one.shape, one.dtype) for one in outs],
        in_specs=[vmem] * 5,
        out_specs=[vmem] * 5,
        compiler_params=pltpu.CompilerParams(vmem_limit_bytes=24 * 2**20),
    )(*outs)
    output, grad_latents, grad_spatial, grad_temporal, grad_cond = outs
    return (
        output.reshape(latents.shape), grad_latents.reshape(latents.shape),
        grad_spatial.reshape(9, chans, chans), grad_temporal.reshape(3, chans, chans), grad_cond)


def solution(mesh):
    return jax.shard_map(
        on_device,
        mesh=mesh,
        in_specs=(
            P("groups", "space", "tm", None, None),
            P("groups", "space", "tm", None, None),
            P("groups"),
            P(),
            P(),
            P(),
        ),
        out_specs=(
            P("groups", "space", "tm", None, None),
            P("groups", "space", "tm", None, None),
            P("groups", None, None),
            P("groups", None, None),
            P("groups", None),
        ),
        check_vma=False,
    )
```

```python
import functools

import jax
import jax.numpy as jnp
from jax import lax
from jax.experimental import pallas as pl
from jax.experimental.pallas import tpu as pltpu
from jax.sharding import PartitionSpec as P

MESH = pl.DeviceIdType.MESH
BF = jnp.bfloat16
F32 = jnp.float32


def nn(left, right):
    return jnp.dot(left, right, preferred_element_type=F32)


def nt(left, right):
    return lax.dot_general(left, right, (((1,), (1,)), ((), ())), preferred_element_type=F32)


def bits_of(count):
    far = []
    bit = 2
    while bit < count:
        far.append(bit)
        bit *= 2
    return far + ([1] if count > 1 else [])


def kernel(n, dims, scale, *refs):
    clips, frames, rows, cols, chans, sizes = dims
    (lat, cotan, mask, sw, tw, cw, out, glat, gsp, gtm, gcd,
     xm, xh, x3, xt, pre, actp, at, cotp, dm, dh, fst, ft, csum, cs, cr, cb,
     acc, tmr, xs, xr, zs, zr, res, swt, twt,
     halo_sem, cot_sem, act_sem, first_sem, sum_sem, tm_sem, x_sem, z_sem,
     g_sem, tg_sem) = refs
    d3 = x3
    group = lax.axis_index("groups")
    s = lax.axis_index("space")
    c = lax.axis_index("tm")
    half = n // 2
    xb = lax.rem(s, 2)
    q = lax.div(s, 2)
    pos = rows * cols
    order = bits_of(n)
    levels = len(order)

    def at_dev(space, core):
        return (group, space, core)

    def copy(src, dst, sems, dev):
        return pltpu.make_async_remote_copy(
            src_ref=src, dst_ref=dst, send_sem=sems[0], recv_sem=sems[1],
            device_id=dev, device_id_type=MESH)

    def pair(sem, *index):
        return sem.at[(0,) + index], sem.at[(1,) + index]

    partner = at_dev(s, 1 - c)
    side = at_dev(s + 1 - 2 * xb, c)

    barrier = pltpu.get_barrier_semaphore()
    pl.semaphore_signal(barrier, inc=1, device_id=partner, device_id_type=MESH)
    for d in range(1, n):
        pl.semaphore_signal(
            barrier, inc=1, device_id=at_dev(lax.rem(s + d, n), c), device_id_type=MESH)
    pl.semaphore_wait(barrier, n)

    def mask_of(b, t):
        return mask[b * frames + t]

    for b in range(clips):
        for t in range(frames):
            cotp[b, t] = (cotan[b, t].astype(F32) * mask_of(b, t)).astype(BF)

    def cot_copy(b):
        return copy(cotp.at[b, pl.ds(0, frames)], cotp.at[b, pl.ds(frames, frames)],
                    pair(cot_sem, b), at_dev(jnp.maximum(s - 1, 0), c))

    def act_copy(b):
        return copy(actp.at[b, pl.ds(frames, frames)], actp.at[b, pl.ds(0, frames)],
                    pair(act_sem, b), at_dev(jnp.minimum(s + 1, n - 1), c))

    @pl.when(s > 0)
    def _():
        for b in range(clips):
            cot_copy(b).start()

    for b in range(clips):
        for t in range(frames):
            xm[b * frames + t] = (lat[b, t].astype(F32) * mask_of(b, t)).astype(BF)

    edge = pl.ds(pl.multiple_of((1 - c) * (rows - 1) * cols, cols), cols)
    x_halo = copy(xm.at[:, edge], xh, pair(halo_sem, 0), partner)
    x_halo.start()

    def d_halo(b):
        span = pl.ds(b * frames, frames)
        return copy(dm.at[span, edge], dh.at[span], pair(halo_sem, 1 + b), partner)

    def clear(upto):
        held = jnp.bool_(True)
        for bit in upto:
            held = held & (lax.rem(lax.div(s, bit), 2) == 0)
        return held

    def has(bit):
        return lax.rem(lax.div(s, bit), 2) == 1

    out_order = order[::-1]

    def first_copy(level, b):
        return copy(fst.at[b], fst.at[b], pair(first_sem, level, b),
                    at_dev(jnp.minimum(s + out_order[level], n - 1), c))

    def first_send(level, b):
        @pl.when(clear(out_order[level:]))
        def _():
            first_copy(level, b).start()

    def first_recv(level, b):
        @pl.when(has(out_order[level]) & clear(out_order[level + 1:]))
        def _():
            first_copy(level, b).wait_recv()

    def first_done(level, b):
        @pl.when(clear(out_order[level:]))
        def _():
            first_copy(level, b).wait_send()

    def sum_copy(level, b):
        return copy(cs.at[b], cr.at[level, b], pair(sum_sem, level, b),
                    at_dev(jnp.maximum(s - order[level], 0), c))

    def sum_send(level, b):
        @pl.when(has(order[level]) & clear(order[:level]))
        def _():
            cs[b] = csum[b].astype(BF)
            sum_copy(level, b).start()

    def sum_recv(level, b):
        @pl.when(clear(order[:level + 1]))
        def _():
            sum_copy(level, b).wait_recv()
            csum[b] += cr[level, b].astype(F32)

    def sum_done(level, b):
        @pl.when(has(order[level]) & clear(order[:level]))
        def _():
            sum_copy(level, b).wait_send()

    hops = sorted(((level, b) for level in range(levels) for b in range(clips)),
                  key=lambda hop: (hop[0] + hop[1], hop[0]))

    def serve(count):
        for _ in range(min(count, len(hops))):
            level, b = hops.pop(0)
            first_recv(level, b)
            if level + 1 < levels:
                first_send(level + 1, b)

    def serve_sum(level):
        for b in range(clips):
            sum_recv(level, b)
            if level + 1 < levels:
                sum_send(level + 1, b)

    @pl.when(s == 0)
    def _():
        for b in range(clips):
            fst[b] = xm[b * frames]

    for b in range(clips):
        first_send(0, b)
        total = cotp[b, 0].astype(F32)
        for t in range(1, frames):
            total += cotp[b, t].astype(F32)
        csum[b] = total
        sum_send(0, b)

    @pl.when(s == n - 1)
    def _():
        cotp[:, frames:] = jnp.zeros((clips, frames, pos, chans), BF)

    @pl.when(s == 0)
    def _():
        actp[:, :frames] = jnp.zeros((clips, frames, pos, chans), BF)

    ids = lax.broadcasted_iota(jnp.int32, (cols, chans), 0)

    def spread(dst, bt, block, value, flip):
        wide = value.astype(F32)
        prev = jnp.where(ids == 0, 0.0, pltpu.roll(wide, 1, 0)).astype(BF)
        nxt = jnp.where(ids == cols - 1, 0.0, pltpu.roll(wide, cols - 1, 0)).astype(BF)
        span = pl.ds(pl.multiple_of(block * cols, cols), cols)
        lo, hi = (nxt, prev) if flip else (prev, nxt)
        dst[bt, span, 0:chans] = lo
        dst[bt, span, chans:2 * chans] = value
        dst[bt, span, 2 * chans:3 * chans] = hi

    def spread_own(dst, src, flip, begin, end):
        @pl.loop(begin, end)
        def _(bt):
            for r in range(rows):
                spread(dst, bt, r + 1, src[bt, r * cols:(r + 1) * cols], flip)

    def spread_halo(dst, src, flip, begin, end):
        @pl.loop(begin, end)
        def _(bt):
            got = src[bt].astype(F32)
            spread(dst, bt, 0, (got * c.astype(F32)).astype(BF), flip)
            spread(dst, bt, rows + 1, (got * (1 - c).astype(F32)).astype(BF), flip)

    spread_own(x3, xm, False, 0, clips * frames)

    @pl.loop(0, clips * frames)
    def _(bt):
        xt[bt] = xm[bt].T

    x_halo.wait()
    spread_halo(x3, xh, False, 0, clips * frames)

    for b in range(clips):
        @pl.loop(0, frames)
        def _(t):
            bt = b * frames + t
            total = nn(x3[bt, 0:pos], sw[0])
            for i in range(1, 3):
                total += nn(x3[bt, i * cols:i * cols + pos], sw[i])
            pre[bt] = total
            act = (total * jax.nn.sigmoid(total)).astype(BF)
            actp[b, frames + t] = act
            at[bt] = act.T

    serve(1)

    for k in range(3):
        twt[k] = tw[k].T
        for j in range(3):
            span = slice(j * chans, (j + 1) * chans)
            swt[k, span] = sw[k, span].T

    base = [sum(sizes[:k]) for k in range(len(sizes))]

    def rows_at(start, size):
        return pl.ds(pl.multiple_of(start, 16), size)

    def tm_copy(k):
        size = sizes[k] // 2
        src = acc.at[rows_at(base[k] + (1 - c) * size, size)]
        return copy(src, tmr.at[pl.ds(base[k] // 2, size)], pair(tm_sem, k), partner)

    zbits = []
    while (1 << len(zbits)) < half:
        zbits.append(1 << len(zbits))

    def z_side(level):
        return lax.rem(lax.div(q, zbits[level]), 2)

    def z_dev(level):
        return at_dev(s + 2 * zbits[level] * (1 - 2 * z_side(level)), c)

    def kept(k, level):
        offset = 0
        for done in range(level):
            offset = offset + z_side(done) * (sizes[k] >> (done + 2))
        return offset

    def z_span(k, level):
        size = sizes[k] >> (level + 2)
        return pl.ds(base[k] // 2 + sizes[k] // 2 - 2 * size, size)

    def z_copy(k, level):
        span = z_span(k, level)
        return copy(zs.at[span], zr.at[span], pair(z_sem, k, level), z_dev(level))

    def x_copy(k):
        span = pl.ds(base[k] // n, sizes[k] // n)
        return copy(xs.at[span], xr.at[span], pair(x_sem, k), side)

    def g_copy(k, level, mine):
        size = sizes[k] >> (level + 2)
        which = z_side(level) if mine else 1 - z_side(level)
        start = base[k] + c * (sizes[k] // 2) + kept(k, level) + which * size
        own = res.at[rows_at(start, size)]
        return copy(own, own, pair(g_sem, k, level), z_dev(level))

    def tg_copy(k, bit):
        size = sizes[k] // 2
        own = res.at[rows_at(base[k] + bit * size, size)]
        return copy(own, own, pair(tg_sem, k), partner)

    def z_send(k, level):
        size = sizes[k] >> (level + 2)
        away = base[k] // 2 + kept(k, level) + (1 - z_side(level)) * size
        zs[z_span(k, level)] = tmr[rows_at(away, size)].astype(BF)
        z_copy(k, level).start()

    def stage_z(k):
        tm_copy(k).wait_recv()
        size = sizes[k] // 2
        span = pl.ds(base[k] // 2, size)
        tmr[span] += acc[rows_at(base[k] + c * size, size)]
        z_send(k, 0)

    def stage_zz(k, level):
        z_copy(k, level - 1).wait_recv()
        size = sizes[k] >> (level + 1)
        span = rows_at(base[k] // 2 + kept(k, level), size)
        tmr[span] += zr[z_span(k, level - 1)].astype(F32)
        if level < len(zbits):
            z_send(k, level)
        else:
            xs[pl.ds(base[k] // n, size)] = tmr[span].astype(BF)
            x_copy(k).start()

    def stage_g(k):
        size = sizes[k] // n
        span = pl.ds(base[k] // n, size)
        x_copy(k).wait_recv()
        total = xs[span].astype(F32) + xr[span].astype(F32)
        start = base[k] + c * (sizes[k] // 2) + kept(k, len(zbits))
        res[rows_at(start, size)] = (total * scale).astype(BF)
        g_copy(k, len(zbits) - 1, True).start()

    def stage_gg(k, level):
        g_copy(k, level, False).wait_recv()
        if level > 0:
            g_copy(k, level - 1, True).start()
        else:
            tg_copy(k, c).start()

    def stage_end(k):
        tg_copy(k, 1 - c).wait_recv()

    for k, taps in enumerate((3, 3, 3, 3, 1)):
        if sizes[k] > taps * chans:
            acc[base[k] + taps * chans:base[k] + sizes[k]] = jnp.zeros(
                (sizes[k] - taps * chans, chans), F32)

    def spatial_grad(b, i):
        @pl.loop(0, 3)
        def _(j):
            total = jnp.zeros((chans, chans), F32)
            for bt in range(b * frames, (b + 1) * frames):
                piece = d3[bt, (2 - i) * cols:(2 - i) * cols + pos,
                           pl.ds(pl.multiple_of(j * chans, chans), chans)]
                total += nn(xt[bt], piece)
            span = pl.ds(pl.multiple_of(base[1 + i] + j * chans, chans), chans)
            if b == 0:
                acc[span] = total
            else:
                acc[span] += total

    def back_sum(b, t):
        bt = b * frames + t
        total = cotp[b, t].astype(F32)
        for i in range(3):
            total += nn(d3[bt, (2 - i) * cols:(2 - i) * cols + pos], swt[i])
        return total

    for b in range(clips):
        @pl.when(s < n - 1)
        def _():
            cot_copy(b).wait_recv()

        if b == clips - 1:
            @pl.when(s < n - 1)
            def _():
                for each in range(clips - 1):
                    act_copy(each).start()

        @pl.loop(0, frames)
        def _(t):
            bt = b * frames + t
            dact = nn(cotp[b, t], twt[0])
            for k in range(1, 3):
                dact += nn(cotp[b, t + k], twt[k])
            value = pre[bt]
            sig = jax.nn.sigmoid(value)
            dm[bt] = (dact * sig * (1.0 + value * (1.0 - sig))).astype(BF)

        d_halo(b).start()

        @pl.loop(0, 3)
        def _(k):
            total = jnp.zeros((chans, chans), F32)
            for t in range(frames):
                total += nn(at[b * frames + t], cotp[b, t + k])
            span = pl.ds(pl.multiple_of(k * chans, chans), chans)
            if b == 0:
                acc[span] = total
            else:
                acc[span] += total

        if b == clips - 1:
            tm_copy(0).start()
        spread_own(d3, dm, True, b * frames, (b + 1) * frames)
        d_halo(b).wait()
        spread_halo(d3, dh, True, b * frames, (b + 1) * frames)
        if b < clips - 1:
            for i in range(3):
                spatial_grad(b, i)
            serve(2)
            if b == 0:
                serve_sum(0)

    last = clips - 1
    deep = len(zbits)

    def middle(k):
        for level in range(1, deep):
            stage_zz(k, level)

    def outer_gather(k):
        for level in range(deep - 1, 0, -1):
            stage_gg(k, level)

    stage_z(0)
    spatial_grad(last, 0)
    tm_copy(1).start()
    serve(2)
    spatial_grad(last, 1)
    tm_copy(2).start()
    stage_z(1)
    spatial_grad(last, 2)
    tm_copy(3).start()
    stage_z(2)
    stage_z(3)

    @pl.when(s < n - 1)
    def _():
        act_copy(last).start()

    for level in range(1, levels - 1):
        serve_sum(level)
    middle(0)
    serve(len(hops))

    total = jnp.zeros((chans, chans), F32)
    for b in range(clips):
        ft[b] = fst[b].T
        for t in range(frames):
            total += nn(ft[b], cotp[b, t])
    acc[base[4]:base[4] + chans] = total
    tm_copy(4).start()
    middle(1)
    stage_zz(0, deep)
    stage_z(4)

    @pl.loop(0, clips)
    def _(b):
        for t in range(1, frames):
            glat[b, t] = (back_sum(b, t) * mask_of(b, t)).astype(BF)

    middle(2)
    stage_zz(1, deep)
    stage_g(0)
    middle(3)

    @pl.loop(0, clips)
    def _(b):
        cb[b] = back_sum(b, 0)

    stage_zz(2, deep)
    stage_g(1)
    stage_zz(3, deep)
    outer_gather(0)
    middle(4)

    @pl.loop(0, clips)
    def _(b):
        cond = nn(fst[b], cw[...])
        for t in range(frames):
            bt = b * frames + t
            total = xm[bt].astype(F32) + cond
            for k in range(t + 1):
                total += nn(actp[b, frames + t - k], tw[k])
            pre[bt] = total

    stage_g(2)
    stage_zz(4, deep)
    stage_gg(0, 0)
    outer_gather(1)
    stage_g(3)
    serve_sum(levels - 1)
    stage_g(4)
    outer_gather(2)

    @pl.when(s == 0)
    def _():
        @pl.loop(0, clips)
        def _(b):
            high = csum[b].astype(BF)
            low = (csum[b] - high.astype(F32)).astype(BF)
            cb[b] += nt(high, cw[...]) + nt(low, cw[...])

    for b in range(clips):
        glat[b, 0] = (cb[b] * mask_of(b, 0)).astype(BF)
    stage_gg(1, 0)
    outer_gather(3)
    outer_gather(4)

    for b in range(clips):
        @pl.when(s > 0)
        def _():
            act_copy(b).wait_recv()

    @pl.loop(0, clips)
    def _(b):
        for t in range(frames):
            bt = b * frames + t
            total = pre[bt]
            for k in range(t + 1, 3):
                total += nn(actp[b, frames + t - k], tw[k])
            out[b, t] = (total * mask_of(b, t)).astype(BF)

    for k in range(2, 5):
        stage_gg(k, 0)
    for k in range(5):
        stage_end(k)
    gtm[...] = res[0:3 * chans]
    gcd[...] = res[base[4]:base[4] + chans]
    for i in range(3):
        gsp[i * 3 * chans:(i + 1) * 3 * chans] = res[base[1 + i]:base[1 + i] + 3 * chans]

    for level in range(levels):
        for b in range(clips):
            first_done(level, b)
            sum_done(level, b)

    @pl.when(s > 0)
    def _():
        for b in range(clips):
            cot_copy(b).wait_send()

    @pl.when(s < n - 1)
    def _():
        for b in range(clips):
            act_copy(b).wait_send()

    for k in range(5):
        tm_copy(k).wait_send()
        x_copy(k).wait_send()
        for level in range(len(zbits)):
            z_copy(k, level).wait_send()
            g_copy(k, level, True).wait_send()
        tg_copy(k, c).wait_send()


def on_device(latents, cotangent, valid_frames, spatial_weight, temporal_weight, cond_weight):
    clips, frames, rows, cols, chans = latents.shape
    n = lax.axis_size("space")
    slab = lax.axis_index("space")
    frame_ids = slab * frames + jnp.arange(frames, dtype=jnp.int32)
    mask = (frame_ids[None, :] < valid_frames[:, None]).astype(F32).reshape(clips * frames)
    scale = (clips * frames * rows * cols * n * lax.axis_size("tm")) ** (-0.5)
    pos = rows * cols
    unit = 16 * n
    sizes = [-(-taps * chans // unit) * unit for taps in (3, 3, 3, 3, 1)]
    total = sum(sizes)
    bt = clips * frames
    levels = len(bits_of(n))
    dma = pltpu.SemaphoreType.DMA
    big = (clips, frames, pos, chans)
    scratch = [
        pltpu.VMEM((bt, pos, chans), BF),
        pltpu.VMEM((bt, cols, chans), BF),
        pltpu.VMEM((bt, pos + 2 * cols, 3 * chans), BF),
        pltpu.VMEM((bt, chans, pos), BF),
        pltpu.VMEM((bt, pos, chans), F32),
        pltpu.VMEM((clips, 2 * frames, pos, chans), BF),
        pltpu.VMEM((bt, chans, pos), BF),
        pltpu.VMEM((clips, 2 * frames, pos, chans), BF),
        pltpu.VMEM((bt, pos, chans), BF),
        pltpu.VMEM((bt, cols, chans), BF),
        pltpu.VMEM((clips, pos, chans), BF),
        pltpu.VMEM((clips, chans, pos), BF),
        pltpu.VMEM((clips, pos, chans), F32),
        pltpu.VMEM((clips, pos, chans), BF),
        pltpu.VMEM((levels, clips, pos, chans), BF),
        pltpu.VMEM((clips, pos, chans), F32),
        pltpu.VMEM((total, chans), F32),
        pltpu.VMEM((total // 2, chans), F32),
        pltpu.VMEM((total // n, chans), BF),
        pltpu.VMEM((total // n, chans), BF),
        pltpu.VMEM((total // 2, chans), BF),
        pltpu.VMEM((total // 2, chans), BF),
        pltpu.VMEM((total, chans), BF),
        pltpu.VMEM((3, 3 * chans, chans), BF),
        pltpu.VMEM((3, chans, chans), BF),
        dma((2, 1 + clips)), dma((2, clips)), dma((2, clips)),
        dma((2, levels, clips)), dma((2, levels, clips)),
        dma((2, 5)), dma((2, 5)), dma((2, 5, levels)), dma((2, 5, levels)), dma((2, 5)),
    ]
    vmem = pl.BlockSpec(memory_space=pltpu.VMEM)
    smem = pl.BlockSpec(memory_space=pltpu.SMEM)
    shape = jax.ShapeDtypeStruct
    outs = pl.pallas_call(
        functools.partial(kernel, n, (clips, frames, rows, cols, chans, sizes), scale),
        out_shape=[
            shape(big, BF), shape(big, BF), shape((9 * chans, chans), BF),
            shape((3 * chans, chans), BF), shape((chans, chans), BF)],
        in_specs=[vmem, vmem, smem, vmem, vmem, vmem],
        out_specs=[vmem] * 5,
        scratch_shapes=scratch,
        compiler_params=pltpu.CompilerParams(
            collective_id=0, has_side_effects=True, vmem_limit_bytes=58 * 2**20),
    )(
        latents.reshape(big), cotangent.reshape(big), mask,
        spatial_weight.reshape(3, 3 * chans, chans), temporal_weight, cond_weight)
    output, grad_latents, grad_spatial, grad_temporal, grad_cond = outs
    return (
        output.reshape(latents.shape), grad_latents.reshape(latents.shape),
        grad_spatial.reshape(9, chans, chans), grad_temporal.reshape(3, chans, chans), grad_cond)


def solution(mesh):
    return jax.shard_map(
        on_device,
        mesh=mesh,
        in_specs=(
            P("groups", "space", "tm", None, None),
            P("groups", "space", "tm", None, None),
            P("groups"),
            P(),
            P(),
            P(),
        ),
        out_specs=(
            P("groups", "space", "tm", None, None),
            P("groups", "space", "tm", None, None),
            P("groups", None, None),
            P("groups", None, None),
            P("groups", None),
        ),
        check_vma=False,
    )
```
